128 devices in a mesh: dom: 16 (over x, z), group: 8 (over y, core).
Axes of the slice: x: 4, y: 4, z: 4, core: 2. Of those that a mesh axis runs over, the one named last changes fastest.
Arguments:
- features: bfloat16 [1114112, 128], P(('dom', 'group')), may hold values from -6 to 6
- tiles: bfloat16 [8704, 8, 128, 128], P(('dom', 'group')), may hold values from 0.049804688 to 1
- tile_src: int32 [8704, 8], P(('dom', 'group')), may hold values from 0 to 131
- send_list: int32 [16, 8, 16, 4], P('dom', 'group'), may hold values from 0 to 67
- w_self: bfloat16 [128, 128], replicated, may hold values from -0.5 to 0.5
- w_neigh: bfloat16 [128, 128], replicated, may hold values from -3 to 3
- gain: float32 [128], replicated, may hold values from 0.25 to 1.75
- shift: float32 [128], replicated, may hold values from -3 to 3
- run_mean: float32 [128], replicated, may hold values from -1 to 1
- run_std: float32 [128], replicated, may hold values from 0.2 to 3
- cotangent: bfloat16 [1114112, 128], P(('dom', 'group')), may hold values from -6 to 6
Outputs:
- output: bfloat16 [1114112, 128], P(('dom', 'group'))
- feature_grad: bfloat16 [1114112, 128], P(('dom', 'group'))
- weight_grad: float32 [256, 128], replicated
- gain_grad: float32 [128], replicated
- shift_grad: float32 [128], replicated
The draws below stay inside these ranges and needn't reach their ends.
All inputs are finite; a program needn't handle non-finite values.
Results may differ from the reference program's by a relative error of at most 0.0051.
Values may be sent and summed in bfloat16 or wider, within the bound.
A program may use at most 256 MiB of HBM per device.

```python
import math
import jax
import jax.numpy as jnp
from jax import lax

F = 128
H = 128
BLK = 128
TILES = 8
BLOCKS_DEV = 68
SENT = 4
NODES = 1114112
N_DOM = 16
N_GROUP = 8


def draw_cotangent(key, part):
    key = jax.random.fold_in(key, 11)
    key_size, key_sign, key_noise = jax.random.split(key, 3)
    magnitude = jax.random.uniform(key_size, (H,), jnp.float32, 1.0, 2.0)
    direction = jnp.where(jax.random.uniform(key_sign, (H,), jnp.float32) < 0.5, -1.0, 1.0)
    offset = magnitude * direction
    noise = jax.random.normal(key_noise, (NODES, H), jnp.float32)
    return jnp.clip(noise + offset[None, :], -6.0, 6.0).astype(jnp.bfloat16)


def with_ends(values, rng, smallest, top_value):
    place = [jax.random.randint(jax.random.fold_in(rng, axis), (), 0, length) for axis, length in enumerate(values.shape)]
    longest = values.shape.index(max(values.shape))
    beside = place[:longest] + [(place[longest] + 1) % values.shape[longest]] + place[longest + 1:]
    return values.at[tuple(place)].set(smallest).at[tuple(beside)].set(top_value)


def steps_of(rng, dims, pieces, smallest, largest):
    level, own = 1.0, jax.random.fold_in(rng, 6)
    for position, blocks in pieces:
        heights = jnp.exp(jax.random.uniform(jax.random.fold_in(own, position), (blocks,), jnp.float32, smallest / len(pieces), largest / len(pieces)))
        level = level * jnp.repeat(heights, dims[position] // blocks).reshape([-1 if axis == position else 1 for axis in range(len(dims))])
    return level


def normal_values(stream_key, dims, spread, reach, cuts=(), kind=jnp.bfloat16):
    drawn = jax.random.normal(stream_key, dims, jnp.float32) * spread
    if len(cuts) > 0:
        drawn = steps_of(stream_key, dims, cuts, -0.22, 0.18) * drawn
    return jnp.clip(drawn, min=-reach, max=reach).astype(kind)


def setup_inputs(seed: int = 0) -> dict:
    arg_keys = jax.random.split(jax.random.key(seed), 12)
    return {
        "features": normal_values(arg_keys[0], (NODES, F), 1.0, 6.0, ((0, 128),)),
        "tiles": jnp.clip(jnp.exp(math.log(1.0) - 2.9996462 * jax.random.uniform(arg_keys[1], (NODES // BLK, TILES, BLK, BLK), jnp.float32) ** steps_of(arg_keys[1], (NODES // BLK, TILES, BLK, BLK), ((0, 128),), -0.2, 0.2)), 0.049804688, 1.0).astype(jnp.bfloat16),
        "tile_src": with_ends(jax.random.randint(arg_keys[2], (NODES // BLK, TILES), 0, BLOCKS_DEV + N_DOM * SENT), jax.random.fold_in(arg_keys[2], 1), 0, (BLOCKS_DEV + N_DOM * SENT) - 1).astype(jnp.int32),
        "send_list": with_ends(jax.random.randint(arg_keys[3], (N_DOM, N_GROUP, N_DOM, SENT), 0, BLOCKS_DEV), jax.random.fold_in(arg_keys[3], 1), 0, BLOCKS_DEV - 1).astype(jnp.int32),
        "w_self": normal_values(arg_keys[4], (F, H), F ** -0.5, 0.5),
        "w_neigh": normal_values(arg_keys[5], (F, H), 0.5, 3.0),
        "gain": jnp.clip(1.0 + 0.15 * jax.random.normal(arg_keys[6], (H,), jnp.float32), 0.25, 1.75),
        "shift": normal_values(arg_keys[7], (H,), 0.5, 3.0, (), jnp.float32),
        "run_mean": jnp.clip(jax.random.uniform(arg_keys[8], (H,), jnp.float32, -1.0, 1.0), -1.0, 1.0),
        "run_std": jnp.clip(jnp.exp(jax.random.uniform(arg_keys[9], (H,), jnp.float32, math.log(0.2), math.log(3.0))), 0.2, 3.0),
        "cotangent": draw_cotangent(jax.random.fold_in(arg_keys[11], 71), 0),
    }


epsilon = 1e-05
clip_ratio = 2.0
clip_shift = 1.0

def reference(features, tiles, tile_src, send_list, w_self, w_neigh, gain, shift, run_mean, run_std, cotangent):
    ndev = N_DOM * N_GROUP
    rows = BLOCKS_DEV * BLK
    node_count_total = float(ndev * rows)
    blocks_all = features.reshape(N_DOM, N_GROUP, BLOCKS_DEV, BLK, F)
    tiles_dev = tiles.reshape(ndev, BLOCKS_DEV, TILES, BLK, BLK)
    source_dev = tile_src.reshape(ndev, BLOCKS_DEV, TILES)
    peers = jnp.arange(N_DOM, dtype=jnp.int32)

    def forward_one(index):
        dom_index = index // N_GROUP
        grp_index = index % N_GROUP
        own = blocks_all[dom_index, grp_index]
        received = blocks_all[peers[:, None], grp_index, send_list[:, grp_index, dom_index, :]]
        pool = jnp.concatenate([own, received.reshape(N_DOM * SENT, BLK, F)], axis=0)
        picked = pool[source_dev[index]]
        tile_here = tiles_dev[index].astype(jnp.float32)
        summed = jnp.einsum('bkij,bkjf->bif', tile_here, picked.astype(jnp.float32))
        degree = lax.optimization_barrier(jnp.sum(tile_here, axis=(1, 3)))
        agg = (summed / degree[:, :, None]).astype(jnp.bfloat16).reshape(rows, F)
        preactivation_here = jnp.dot(own.reshape(rows, F), w_self, preferred_element_type=jnp.float32) + jnp.dot(agg, w_neigh, preferred_element_type=jnp.float32)
        return (agg, degree, preactivation_here)
    agg_all, degree_all, preactivation_full = lax.map(forward_one, jnp.arange(ndev, dtype=jnp.int32))
    batch_mean_value = lax.optimization_barrier(jnp.sum(preactivation_full, axis=(0, 1))) / node_count_total
    var_val = lax.optimization_barrier(jnp.sum((preactivation_full - batch_mean_value) ** 2, axis=(0, 1))) / node_count_total
    batch_stddev = jnp.sqrt(var_val + epsilon)
    renorm_ratio = jnp.clip(batch_stddev / run_std, 1.0 / clip_ratio, clip_ratio)
    renorm_offset = jnp.clip((batch_mean_value - run_mean) / run_std, -clip_shift, clip_shift)
    normalized_input = (preactivation_full - batch_mean_value) / batch_stddev
    layer_output_value = normalized_input * renorm_ratio + renorm_offset
    pre = gain * layer_output_value + shift
    sigmoid_value = jax.nn.sigmoid(pre)
    output = (pre * sigmoid_value).astype(jnp.bfloat16).reshape(ndev * rows, H)
    grad_in = cotangent.astype(jnp.float32).reshape(ndev, rows, H)
    grad_y = grad_in * sigmoid_value * (1.0 + pre * (1.0 - sigmoid_value))
    gain_grad = lax.optimization_barrier(jnp.sum(grad_y * layer_output_value, axis=(0, 1)))
    shift_grad = lax.optimization_barrier(jnp.sum(grad_y, axis=(0, 1)))
    normalized_input_gradient = grad_y * gain * renorm_ratio
    mean_moment_sum = lax.optimization_barrier(jnp.sum(normalized_input_gradient, axis=(0, 1))) / node_count_total
    square_moment_sum = lax.optimization_barrier(jnp.sum(normalized_input_gradient * normalized_input, axis=(0, 1))) / node_count_total
    preact_gradient_full = (normalized_input_gradient - mean_moment_sum - normalized_input * square_moment_sum) / batch_stddev

    def backward_one(index):
        dom_index = index // N_GROUP
        grp_index = index % N_GROUP
        own = blocks_all[dom_index, grp_index].reshape(rows, F)
        stacked = jnp.concatenate([own, agg_all[index]], axis=1).astype(jnp.float32)
        dz_here = preact_gradient_full[index]
        wgrad = jnp.dot(stacked.T, dz_here, precision=lax.Precision.HIGHEST)
        dz_low = dz_here.astype(jnp.bfloat16)
        dself = jnp.dot(dz_low, w_self.T, preferred_element_type=jnp.float32)
        dagg = jnp.dot(dz_low, w_neigh.T, preferred_element_type=jnp.float32)
        scaled = (dagg.reshape(BLOCKS_DEV, BLK, F) / degree_all[index][:, :, None]).astype(jnp.bfloat16)
        contrib = jnp.einsum('bkij,bif->bkjf', tiles_dev[index].astype(jnp.float32), scaled.astype(jnp.float32))
        pool_grad = jnp.zeros((BLOCKS_DEV + N_DOM * SENT, BLK, F), jnp.float32)
        pool_grad = pool_grad.at[source_dev[index].reshape(-1)].add(contrib.reshape(-1, BLK, F))
        partial_sum = dself.reshape(BLOCKS_DEV, BLK, F) + pool_grad[:BLOCKS_DEV]
        remote = pool_grad[BLOCKS_DEV:].reshape(N_DOM, SENT, BLK, F).astype(jnp.bfloat16)
        return (wgrad, partial_sum, remote)
    wgrads, partial_all, remote_all = lax.map(backward_one, jnp.arange(ndev, dtype=jnp.int32))
    weight_grad = lax.optimization_barrier(jnp.sum(wgrads, axis=0))
    remote_view = remote_all.reshape(N_DOM, N_GROUP, N_DOM, SENT, BLK, F)

    def finish_one(index):
        dom_index = index // N_GROUP
        grp_index = index % N_GROUP
        back = remote_view[:, grp_index, dom_index].astype(jnp.float32)
        returned = jnp.zeros((BLOCKS_DEV, BLK, F), jnp.float32)
        returned = returned.at[send_list[dom_index, grp_index].reshape(-1)].add(back.reshape(-1, BLK, F))
        return (partial_all[index] + returned).astype(jnp.bfloat16)
    feature_grad = lax.map(finish_one, jnp.arange(ndev, dtype=jnp.int32)).reshape(ndev * rows, F)
    return (output, feature_grad, weight_grad, gain_grad, shift_grad)
```

```python
import functools

import jax
import jax.numpy as jnp
from jax import lax
from jax.experimental import pallas as pl
from jax.experimental.pallas import tpu as pltpu
from jax.sharding import PartitionSpec as P

BLK = 128
TILES = 8
NB = 68
SENT = 4
NDOM = 16
NGRP = 8
NREM = NDOM * SENT
NT = NB * TILES
NPOOL = NB + NREM
PAIRS_REMOTE = (NT + NREM) // 2
PAIRS = (NT + NPOOL) // 2
POS_ROWS = 6
SEG = 256
ROWS = NB * BLK
MESH = pl.DeviceIdType.MESH
F32 = jnp.float32
BF16 = jnp.bfloat16

epsilon = 1e-05
clip_ratio = 2.0
clip_shift = 1.0

OFFSETS = (
    (2, 2), (2, 1), (1, 2), (2, 3), (3, 2), (1, 1), (3, 3), (1, 3),
    (3, 1), (2, 0), (0, 2), (1, 0), (0, 1), (3, 0), (0, 3),
)

C_TILE, C_BLOCK, C_KEEP, C_END = 0, 6, 12, 15
C_BACK, C_BKEEP, C_BEND = 17, 18, 19
C_SRC, C_LIST = 24, 32
C_ROWS = 40


def fiota(shape, dim):
    return lax.broadcasted_iota(jnp.int32, shape, dim).astype(F32)


def lane_sum(v):
    return jnp.sum(v, axis=1, keepdims=True)


def row_sum(v):
    return jnp.sum(v, axis=0, keepdims=True)


def one(mask):
    return jnp.where(mask, 1.0, 0.0)


def plan_order(cols, rows, nseg, group):
    n = len(cols)
    lanes = fiota((BLK, nseg), 1)
    counts_row = row_sum(sum(one(c == lanes) for c in cols))
    subl = fiota((nseg, BLK), 0)
    counts_col = lane_sum(sum(one(r == subl) for r in rows))
    groups_row = jnp.floor((counts_row + (group - 1)) * (1.0 / group))
    groups_col = jnp.floor((counts_col + (group - 1)) * (1.0 / group))
    up = fiota((nseg, nseg), 0)
    across = fiota((nseg, nseg), 1)
    start_row = row_sum(jnp.where(up < across, groups_col, 0.0))
    start_col = lane_sum(jnp.where(across < up, groups_row, 0.0))
    earlier = fiota((BLK, BLK), 1) < fiota((BLK, BLK), 0)
    places = []
    for k in range(n):
        same = sum((one(rows[j] == cols[k]) for j in range(k)), jnp.zeros((BLK, BLK), F32))
        same = same + one((rows[k] == cols[k]) & earlier)
        start = lane_sum(jnp.where(cols[k] == lanes, start_row, 0.0))
        place = start * group + lane_sum(same)
        places.append(jnp.where(cols[k] < nseg, place, -1.0))
    return start_row, start_col, groups_row, counts_row, counts_col, places


def put_rows(ctl, first, values):
    width = values.shape[1]
    for i in range(width // BLK):
        ctl[first + i : first + i + 1, :] = values[:, i * BLK : (i + 1) * BLK].astype(jnp.int32)


def plan(srct, listt, ctl, wide):
    ctl[...] = jnp.zeros_like(ctl)
    ctl[C_SRC : C_SRC + TILES, 0:NB] = srct[...]
    ctl[C_LIST : C_LIST + SENT, 0:NDOM] = listt[...]
    wide[...] = jnp.full(wide.shape, 1000.0, F32)
    s = srct[...].astype(F32)
    wide[0:TILES, 0:NB] = jnp.where(s >= NB, s - NB, s + NREM)
    st = wide[...]
    s = st.T
    cols = [s[:, k : k + 1] for k in range(TILES)]
    rows = [st[k : k + 1, :] for k in range(TILES)]
    start_row, start_col, groups_row, counts_row, counts_col, places = plan_order(cols, rows, SEG, 2)
    node = fiota((BLK, POS_ROWS * BLK), 0)
    spot = fiota((BLK, POS_ROWS * BLK), 1)
    held = row_sum(
        sum(jnp.where(places[k] == spot, node * TILES + (k + 1.0), 0.0) for k in range(TILES))
    )
    item = jnp.maximum(held - 1.0, 0.0)
    put_rows(ctl, C_TILE, item)
    put_rows(ctl, C_BLOCK, jnp.where(held > 0.0, jnp.floor(item * (1.0 / TILES)), float(NB)))
    spots = fiota((SEG, 3 * BLK), 1)
    first = row_sum(jnp.where((start_col == spots) & (counts_col > 0.0), 1.0, 0.0))
    put_rows(ctl, C_KEEP, 1.0 - first)
    put_rows(ctl, C_END, jnp.where(counts_row > 0.0, start_row + groups_row - 1.0, -1.0))

    wide[...] = jnp.full(wide.shape, 1000.0, F32)
    wide[0:SENT, 0:NDOM] = listt[...].astype(F32)
    bt = wide[...]
    b = bt.T
    cols = [b[:, k : k + 1] for k in range(SENT)]
    rows = [bt[k : k + 1, :] for k in range(SENT)]
    start_row, start_col, groups_row, counts_row, counts_col, places = plan_order(cols, rows, BLK, 1)
    node = fiota((BLK, BLK), 0)
    spot = fiota((BLK, BLK), 1)
    put_rows(ctl, C_BACK, row_sum(sum(jnp.where(places[k] == spot, node * SENT + k, 0.0) for k in range(SENT))))
    first = row_sum(jnp.where((start_col == spot) & (counts_col > 0.0), 1.0, 0.0))
    put_rows(ctl, C_BKEEP, 1.0 - first)
    put_rows(ctl, C_BEND, jnp.where(counts_row > 0.0, start_row + groups_row - 1.0, -1.0))


def finish(out_a, fg_a, wg_a, gg_a, sg_a, out, fg, wg, gg, sg, sem):
    pieces = 4
    n = NB // pieces
    cps = []
    for i in range(pieces):
        cut = pl.ds(i * n, n)
        cps.append(pltpu.make_async_copy(out_a.at[cut], out.at[cut], sem.at[2 * i]))
        cps.append(pltpu.make_async_copy(fg_a.at[cut], fg.at[cut], sem.at[2 * i + 1]))
    for cp in cps:
        cp.start()
    wg[...] = wg_a[...]
    gg[...] = gg_a[...]
    sg[...] = sg_a[...]
    for cp in cps:
        cp.wait()


def fold(v):
    return jnp.sum(v.reshape(-1, 8, v.shape[-1]), axis=0)


def layer(
    cs, feat_h, tiles_h, cot_h, wself, wneigh, gain, shift, rmean, rstd,
    out_h, fg_h, wg_out, gg_out, sg_out,
    tv, pool, own, st, back, agg, ct, inv, ost, slots, wloc, wgat, wdom, ga, da, gb, db,
    lsem, tsem, osem, fsend, frecv, bsend, brecv, gs, gr, ds, dr, w1s, w1r, w2s, w2r, w3s, w3r,
):
    d = lax.axis_index("dom")
    g = lax.axis_index("group")
    x = d // 4
    zc = d % 4

    def dpeer(off):
        return ((x + off[0]) % 4) * 4 + (zc + off[1]) % 4

    load_feat = pltpu.make_async_copy(feat_h, own, lsem.at[0])
    load_tiles = pltpu.make_async_copy(tiles_h, tv, tsem.at[0])
    load_cot = pltpu.make_async_copy(cot_h, ct, lsem.at[1])
    load_feat.start()
    barrier = pltpu.get_barrier_semaphore()
    for off in OFFSETS:
        pl.semaphore_signal(barrier, inc=1, device_id=(dpeer(off), g), device_id_type=MESH)
    for k in range(1, NGRP):
        pl.semaphore_signal(barrier, inc=1, device_id=(d, (g + k) % NGRP), device_id_type=MESH)
    load_feat.wait()
    load_tiles.start()
    load_cot.start()

    def forward_copy(i):
        return pltpu.make_async_remote_copy(
            src_ref=st.at[pl.ds(i * SENT, SENT)],
            dst_ref=pool.at[pl.ds(NB + d * SENT, SENT)],
            send_sem=fsend.at[i],
            recv_sem=frecv.at[i],
            device_id=(dpeer(OFFSETS[i]), g),
            device_id_type=MESH,
        )

    def backward_copy(i):
        return pltpu.make_async_remote_copy(
            src_ref=st.at[pl.ds(i * SENT, SENT)],
            dst_ref=back.at[pl.ds(d * SENT, SENT)],
            send_sem=bsend.at[i],
            recv_sem=brecv.at[i],
            device_id=(dpeer(OFFSETS[i]), g),
            device_id_type=MESH,
        )

    npeers = len(OFFSETS)
    for i in range(npeers):
        p = dpeer(OFFSETS[i])
        for s in range(SENT):
            st[i * SENT + s] = own[cs[C_LIST + s, p]]
        if i == 0:
            pl.semaphore_wait(barrier, npeers + NGRP - 1)
        forward_copy(i).start()

    for s in range(SENT):
        pool[NB + d * SENT + s] = own[cs[C_LIST + s, d]]

    @pl.loop(0, NB, unroll=4)
    def _(b):
        pool[b] = own[b]

    z = slots.at[pl.ds(0, NB)]
    gy = slots.at[pl.ds(NB, NB)]
    w1 = wself[...]
    w2 = wneigh[...]

    @pl.loop(0, NB // 4)
    def _(c):
        rows = own[pl.ds(c * 4, 4)].reshape(4 * BLK, BLK)
        z[pl.ds(c * 4, 4)] = jnp.dot(rows, w1, preferred_element_type=F32).reshape(4, BLK, BLK)

    load_tiles.wait()
    ones = jnp.ones((TILES * BLK, BLK), BF16)

    @pl.loop(0, NB, unroll=4)
    def _(b):
        left = jnp.concatenate([tv[b * TILES + k] for k in range(TILES)], axis=1)
        inv[b] = 1.0 / jnp.dot(left, ones, preferred_element_type=F32)

    load_cot.wait()
    for i in range(npeers):
        forward_copy(i).wait_recv()

    @pl.loop(0, NB, unroll=17)
    def _(b):
        left = jnp.concatenate([tv[b * TILES + k] for k in range(TILES)], axis=1)
        right = jnp.concatenate([pool[cs[C_SRC + k, b]] for k in range(TILES)], axis=0)
        summed = jnp.dot(left, right, preferred_element_type=F32)
        agg[b] = (summed * inv[b]).astype(BF16)

    def project(c, total):
        rows = agg[pl.ds(c * 4, 4)].reshape(4 * BLK, BLK)
        zz = z[pl.ds(c * 4, 4)].reshape(4 * BLK, BLK) + jnp.dot(rows, w2, preferred_element_type=F32)
        z[pl.ds(c * 4, 4)] = zz.reshape(4, BLK, BLK)
        return total + fold(zz)

    zero8 = jnp.zeros((8, BLK), F32)
    total = lax.fori_loop(0, NB // 4, project, zero8)
    mean_here = row_sum(total) * (1.0 / ROWS)

    def squares(b, total):
        c = z[b] - mean_here
        return total + fold(c * c)

    square_here = row_sum(lax.fori_loop(0, NB, squares, zero8, unroll=4))

    def group_copies(n, buf):
        cps = []
        for k in range(1, NGRP):
            to = (g + k) % NGRP
            cps.append(pltpu.make_async_remote_copy(
                src_ref=buf.at[g], dst_ref=buf.at[g], send_sem=gs.at[n, k], recv_sem=gr.at[n, k],
                device_id=(d, to), device_id_type=MESH,
            ))
        return cps

    def dom_copies(n, buf):
        cps = []
        for k in range(npeers):
            cps.append(pltpu.make_async_remote_copy(
                src_ref=buf.at[d], dst_ref=buf.at[d], send_sem=ds.at[n, k], recv_sem=dr.at[n, k],
                device_id=(dpeer(OFFSETS[k]), g), device_id_type=MESH,
            ))
        return cps

    def merge(buf, count, n):
        means = jnp.sum(buf[:, 0:1, :], axis=0) * (1.0 / count)
        spread = jnp.sum((buf[:, 0:1, :] - means[None]) ** 2, axis=0)
        return means, jnp.sum(buf[:, 1:2, :], axis=0) + spread * n

    ga[g] = jnp.concatenate([mean_here, square_here], axis=0)
    ga_cps = group_copies(0, ga)
    for cp in ga_cps:
        cp.start()
    for cp in ga_cps:
        cp.wait_recv()
    mean_g, square_g = merge(ga, NGRP, float(ROWS))
    da[d] = jnp.concatenate([mean_g, square_g], axis=0)
    da_cps = dom_copies(0, da)
    for cp in da_cps:
        cp.start()
    for i in range(npeers):
        forward_copy(i).wait_send()
    for cp in ga_cps:
        cp.wait_send()
    for cp in da_cps:
        cp.wait_recv()
    mu, square_all = merge(da, NDOM, float(ROWS * NGRP))
    nodes = float(ROWS * NGRP * NDOM)
    sigma = jnp.sqrt(square_all * (1.0 / nodes) + epsilon)
    isg = 1.0 / sigma
    rs = rstd[...]
    gn = gain[...]
    ratio = jnp.clip(sigma / rs, 1.0 / clip_ratio, clip_ratio)
    offset = jnp.clip((mu - rmean[...]) / rs, -clip_shift, clip_shift)
    slope = gn * ratio
    bias = gn * offset + shift[...]

    def activate(b, sums):
        xh = (z[b] - mu) * isg
        pre = xh * slope + bias
        sg = 1.0 / (1.0 + jnp.exp(-pre))
        ost[b] = (pre * sg).astype(BF16)
        dy = ct[b].astype(F32) * sg * (1.0 + pre * (1.0 - sg))
        gy[b] = dy
        return sums[0] + fold(dy), sums[1] + fold(dy * xh)

    sum_gy, sum_gx = lax.fori_loop(0, NB, activate, (zero8, zero8), unroll=2)
    write_out = pltpu.make_async_copy(ost, out_h, osem.at[0])
    write_out.start()

    gb[g] = jnp.concatenate([row_sum(sum_gy), row_sum(sum_gx)], axis=0)
    gb_cps = group_copies(1, gb)
    for cp in gb_cps:
        cp.start()
    for cp in gb_cps:
        cp.wait_recv()
    db[d] = jnp.sum(gb[...], axis=0)
    db_cps = dom_copies(1, db)
    for cp in db_cps:
        cp.start()
    for cp in da_cps:
        cp.wait_send()
    for cp in gb_cps:
        cp.wait_send()
    write_out.wait()
    for cp in db_cps:
        cp.wait_recv()
    sums = jnp.sum(db[...], axis=0)
    sum_gy = sums[0:1]
    sum_gx = sums[1:2]
    gg_out[...] = ratio * sum_gx + offset * sum_gy
    sg_out[...] = sum_gy
    k1 = slope * isg
    k2 = k1 * sum_gy * (1.0 / nodes)
    k3 = k1 * sum_gx * (1.0 / nodes)

    @pl.loop(0, NB, unroll=4)
    def _(b):
        xh = (z[b] - mu) * isg
        dz = gy[b] * k1 - k2 - xh * k3
        hi = dz.astype(BF16)
        ct[b] = hi
        ost[b] = (dz - hi.astype(F32)).astype(BF16)
        dagg = lax.dot_general(hi, w2, (((1,), (1,)), ((), ())), preferred_element_type=F32)
        pool[b] = (dagg * inv[b]).astype(BF16)

    pool[NB] = jnp.zeros((BLK, BLK), BF16)

    def pair(p, acc):
        left = jnp.concatenate([tv[cs[C_TILE + (2 * p + j) // BLK, (2 * p + j) % BLK]] for j in range(2)], axis=0)
        right = jnp.concatenate([pool[cs[C_BLOCK + (2 * p + j) // BLK, (2 * p + j) % BLK]] for j in range(2)], axis=0)
        part = lax.dot_general(left, right, (((0,), (0,)), ((), ())), preferred_element_type=F32)
        keep = cs[C_KEEP + p // BLK, p % BLK].astype(F32)
        acc = acc * keep + part
        slots[p] = acc
        return acc

    lax.fori_loop(0, PAIRS_REMOTE, pair, jnp.zeros((BLK, BLK), F32), unroll=8)

    def ended(q):
        e = cs[C_END + q // BLK, q % BLK]
        return jnp.where(e >= 0, slots[jnp.maximum(e, 0)], 0.0)

    for i in range(npeers):
        p = dpeer(OFFSETS[i])
        for s in range(SENT):
            st[i * SENT + s] = ended(p * SENT + s).astype(BF16)
        backward_copy(i).start()
    for s in range(SENT):
        back[d * SENT + s] = ended(d * SENT + s).astype(BF16)

    def weight(c, acc):
        left = jnp.concatenate(
            [own[pl.ds(c * 4, 4)].reshape(4 * BLK, BLK), agg[pl.ds(c * 4, 4)].reshape(4 * BLK, BLK)], axis=1
        )
        right = jnp.concatenate(
            [ct[pl.ds(c * 4, 4)].reshape(4 * BLK, BLK), ost[pl.ds(c * 4, 4)].reshape(4 * BLK, BLK)], axis=1
        )
        wloc[...] += lax.dot_general(left, right, (((0,), (0,)), ((), ())), preferred_element_type=F32)
        return acc

    wloc[...] = jnp.zeros_like(wloc)
    lax.fori_loop(0, NB // 4, weight, 0)
    part = 2 * BLK // NGRP
    wsum = wloc[:, :BLK] + wloc[:, BLK:]
    wloc[:, :BLK] = wsum
    w1_cps = []
    for k in range(1, NGRP):
        to = (g + k) % NGRP
        w1_cps.append(pltpu.make_async_remote_copy(
            src_ref=wloc.at[pl.ds(to * part, part), pl.ds(0, BLK)], dst_ref=wgat.at[g], send_sem=w1s.at[k], recv_sem=w1r.at[k],
            device_id=(d, to), device_id_type=MESH,
        ))
    for cp in w1_cps:
        cp.start()
    wgat[g] = wloc[pl.ds(g * part, part), pl.ds(0, BLK)]

    last = slots[PAIRS_REMOTE - 1]
    lax.fori_loop(PAIRS_REMOTE, PAIRS, pair, last, unroll=2)

    for cp in w1_cps:
        cp.wait_recv()
    wdom[d] = jnp.sum(wgat[...], axis=0)
    w2_cps = []
    for k in range(npeers):
        w2_cps.append(pltpu.make_async_remote_copy(
            src_ref=wdom.at[d], dst_ref=wdom.at[d], send_sem=w2s.at[k], recv_sem=w2r.at[k],
            device_id=(dpeer(OFFSETS[k]), g), device_id_type=MESH,
        ))
    for cp in w2_cps:
        cp.start()

    @pl.loop(0, NB, unroll=4)
    def _(b):
        dself = lax.dot_general(ct[b], w1, (((1,), (1,)), ((), ())), preferred_element_type=F32)
        inv[b] = dself + ended(NREM + b)

    for cp in w2_cps:
        cp.wait_recv()
    wg_out[pl.ds(g * part, part)] = jnp.sum(wdom[...], axis=0)
    w3_cps = []
    for k in range(1, NGRP):
        w3_cps.append(pltpu.make_async_remote_copy(
            src_ref=wg_out.at[pl.ds(g * part, part)], dst_ref=wg_out.at[pl.ds(g * part, part)],
            send_sem=w3s.at[k], recv_sem=w3r.at[k], device_id=(d, (g + k) % NGRP), device_id_type=MESH,
        ))
    for cp in w3_cps:
        cp.start()

    for i in range(npeers):
        backward_copy(i).wait_recv()

    def gather_back(n, acc):
        keep = cs[C_BKEEP, n].astype(F32)
        acc = acc * keep + back[cs[C_BACK, n]].astype(F32)
        slots[n] = acc
        return acc

    lax.fori_loop(0, NREM, gather_back, jnp.zeros((BLK, BLK), F32), unroll=4)

    @pl.loop(0, NB, unroll=4)
    def _(b):
        e = cs[C_BEND, b]
        agg[b] = (inv[b] + jnp.where(e >= 0, slots[jnp.maximum(e, 0)], 0.0)).astype(BF16)

    write_fg = pltpu.make_async_copy(agg, fg_h, osem.at[1])
    write_fg.start()
    for cp in w3_cps:
        cp.wait_recv()
    for i in range(npeers):
        backward_copy(i).wait_send()
    for cp in db_cps + w1_cps + w2_cps + w3_cps:
        cp.wait_send()
    write_fg.wait()


def on_device(features, tiles, tile_src, send_list, w_self, w_neigh, gain, shift, run_mean, run_std, cotangent):
    vm = pl.BlockSpec(memory_space=pltpu.VMEM)
    sm = pl.BlockSpec(memory_space=pltpu.SMEM)
    hb = pl.BlockSpec(memory_space=pl.ANY)
    dma = pltpu.SemaphoreType.DMA
    part = 2 * BLK // NGRP
    ctl = pl.pallas_call(
        plan,
        name="plan",
        out_shape=jax.ShapeDtypeStruct((C_ROWS, BLK), jnp.int32),
        in_specs=[vm, vm],
        out_specs=vm,
        scratch_shapes=[pltpu.VMEM((BLK, BLK), F32)],
    )(tile_src.T, send_list.reshape(NDOM, SENT).T)
    results = (
        jax.ShapeDtypeStruct((NB, BLK, BLK), BF16),
        jax.ShapeDtypeStruct((NB, BLK, BLK), BF16),
        jax.ShapeDtypeStruct((2 * BLK, BLK), F32),
        jax.ShapeDtypeStruct((1, BLK), F32),
        jax.ShapeDtypeStruct((1, BLK), F32),
    )
    made = pl.pallas_call(
        layer,
        name="sage",
        out_shape=results,
        in_specs=[sm, hb, hb, hb] + [vm] * 6,
        out_specs=(hb, hb, vm, vm, vm),
        scratch_shapes=[
            pltpu.VMEM((NT, BLK, BLK), BF16),
            pltpu.VMEM((NPOOL, BLK, BLK), BF16),
            pltpu.VMEM((NB, BLK, BLK), BF16),
            pltpu.VMEM((NREM, BLK, BLK), BF16),
            pltpu.VMEM((NREM, BLK, BLK), BF16),
            pltpu.VMEM((NB, BLK, BLK), BF16),
            pltpu.VMEM((NB, BLK, BLK), BF16),
            pltpu.VMEM((NB, BLK, BLK), F32),
            pltpu.VMEM((NB, BLK, BLK), BF16),
            pltpu.VMEM((PAIRS, BLK, BLK), F32),
            pltpu.VMEM((2 * BLK, 2 * BLK), F32),
            pltpu.VMEM((NGRP, part, BLK), F32),
            pltpu.VMEM((NDOM, part, BLK), F32),
            pltpu.VMEM((NGRP, 2, BLK), F32),
            pltpu.VMEM((NDOM, 2, BLK), F32),
            pltpu.VMEM((NGRP, 2, BLK), F32),
            pltpu.VMEM((NDOM, 2, BLK), F32),
            dma((2,)), dma((1,)), dma((2,)),
            dma((15,)), dma((15,)), dma((15,)), dma((15,)),
            dma((2, 8)), dma((2, 8)), dma((2, 15)), dma((2, 15)),
            dma((8,)), dma((8,)), dma((15,)), dma((15,)), dma((8,)), dma((8,)),
        ],
        compiler_params=pltpu.CompilerParams(
            collective_id=1, has_side_effects=True, vmem_limit_bytes=63 * 1024 * 1024
        ),
    )(
        ctl,
        features.reshape(NB, BLK, BLK), tiles.reshape(NT, BLK, BLK), cotangent.reshape(NB, BLK, BLK),
        w_self, w_neigh, gain.reshape(1, BLK), shift.reshape(1, BLK), run_mean.reshape(1, BLK), run_std.reshape(1, BLK),
    )
    out, fg, wg, gg, sg = pl.pallas_call(
        finish,
        name="finish",
        out_shape=results,
        in_specs=[hb, hb, vm, vm, vm],
        out_specs=(hb, hb, vm, vm, vm),
        scratch_shapes=[dma((8,))],
    )(*made)
    return out.reshape(ROWS, BLK), fg.reshape(ROWS, BLK), wg, gg.reshape(BLK), sg.reshape(BLK)


def solution(mesh):
    rows = P(("dom", "group"), None)
    return jax.shard_map(
        on_device,
        mesh=mesh,
        in_specs=(
            rows,
            P(("dom", "group"), None, None, None),
            rows,
            P("dom", "group", None, None),
            P(), P(), P(), P(), P(), P(),
            rows,
        ),
        out_specs=(rows, rows, P(), P(), P()),
        check_vma=False,
    )
```

```python
import functools

import jax
import jax.numpy as jnp
from jax import lax
from jax.experimental import pallas as pl
from jax.experimental.pallas import tpu as pltpu
from jax.sharding import PartitionSpec as P

BLK = 128
TILES = 8
NB = 68
SENT = 4
NDOM = 16
NGRP = 8
NREM = NDOM * SENT
NT = NB * TILES
NPOOL = NB + NREM
PAIRS_REMOTE = (NT + NREM) // 2
PAIRS = (NT + NPOOL) // 2
POS_ROWS = 6
SEG = 256
ROWS = NB * BLK
MESH = pl.DeviceIdType.MESH
F32 = jnp.float32
BF16 = jnp.bfloat16

epsilon = 1e-05
clip_ratio = 2.0
clip_shift = 1.0

OFFSETS = (
    (2, 2), (2, 1), (1, 2), (2, 3), (3, 2), (1, 1), (3, 3), (1, 3),
    (3, 1), (2, 0), (0, 2), (1, 0), (0, 1), (3, 0), (0, 3),
)

C_TILE, C_KEEP, C_END, C_SRC, C_LIST = 0, 6, 9, 16, 24
C_ROWS = 32


def fiota(shape, dim):
    return lax.broadcasted_iota(jnp.int32, shape, dim).astype(F32)


def lane_sum(v):
    return jnp.sum(v, axis=1, keepdims=True)


def row_sum(v):
    return jnp.sum(v, axis=0, keepdims=True)


def one(mask):
    return jnp.where(mask, 1.0, 0.0)


def plan_order(cols, rows, nseg, group):
    n = len(cols)
    lanes = fiota((BLK, nseg), 1)
    counts_row = row_sum(sum(one(c == lanes) for c in cols))
    subl = fiota((nseg, BLK), 0)
    counts_col = lane_sum(sum(one(r == subl) for r in rows))
    groups_row = jnp.floor((counts_row + (group - 1)) * (1.0 / group))
    groups_col = jnp.floor((counts_col + (group - 1)) * (1.0 / group))
    up = fiota((nseg, nseg), 0)
    across = fiota((nseg, nseg), 1)
    start_row = row_sum(jnp.where(up < across, groups_col, 0.0))
    start_col = lane_sum(jnp.where(across < up, groups_row, 0.0))
    earlier = fiota((BLK, BLK), 1) < fiota((BLK, BLK), 0)
    places = []
    for k in range(n):
        same = sum((one(rows[j] == cols[k]) for j in range(k)), jnp.zeros((BLK, BLK), F32))
        same = same + one((rows[k] == cols[k]) & earlier)
        start = lane_sum(jnp.where(cols[k] == lanes, start_row, 0.0))
        place = start * group + lane_sum(same)
        places.append(jnp.where(cols[k] < nseg, place, -1.0))
    return start_row, start_col, groups_row, counts_row, counts_col, places


def put_rows(ctl, first, values):
    width = values.shape[1]
    for i in range(width // BLK):
        ctl[first + i : first + i + 1, :] = values[:, i * BLK : (i + 1) * BLK].astype(jnp.int32)


def plan(srct, listt, ctl, wide):
    ctl[...] = jnp.zeros_like(ctl)
    ctl[C_SRC : C_SRC + TILES, 0:NB] = srct[...]
    ctl[C_LIST : C_LIST + SENT, 0:NDOM] = listt[...]
    wide[...] = jnp.full(wide.shape, 1000.0, F32)
    s = srct[...].astype(F32)
    wide[0:TILES, 0:NB] = jnp.where(s >= NB, s - NB, s + NREM)
    st = wide[...]
    s = st.T
    cols = [s[:, k : k + 1] for k in range(TILES)]
    rows = [st[k : k + 1, :] for k in range(TILES)]
    start_row, start_col, groups_row, counts_row, counts_col, places = plan_order(cols, rows, SEG, 2)
    node = fiota((BLK, POS_ROWS * BLK), 0)
    spot = fiota((BLK, POS_ROWS * BLK), 1)
    held = row_sum(
        sum(jnp.where(places[k] == spot, node * TILES + (k + 1.0), 0.0) for k in range(TILES))
    )
    put_rows(ctl, C_TILE, jnp.where(held > 0.0, held - 1.0, float(NT)))
    spots = fiota((SEG, 3 * BLK), 1)
    first = row_sum(jnp.where((start_col == spots) & (counts_col > 0.0), 1.0, 0.0))
    put_rows(ctl, C_KEEP, 1.0 - first)
    put_rows(ctl, C_END, jnp.where(counts_row > 0.0, start_row + groups_row - 1.0, -1.0))


def finish(
    cs, out_a, part_a, back_a, wg_a, gg_a, sg_a, out, fg, wg, gg, sg, held, part, back, made, psem, bsem, isem, osem, fsem
):
    n = NB // 4
    cuts = [pl.ds(i * n, n) for i in range(4)]
    load_back = pltpu.make_async_copy(back_a, back, bsem.at[0])
    load_part = [pltpu.make_async_copy(part_a.at[c], part.at[c], psem.at[i]) for i, c in enumerate(cuts)]
    load_out = [pltpu.make_async_copy(out_a.at[c], held.at[c], isem.at[i]) for i, c in enumerate(cuts)]
    put_out = [pltpu.make_async_copy(held.at[c], out.at[c], osem.at[i]) for i, c in enumerate(cuts)]
    put_fg = [pltpu.make_async_copy(made.at[c], fg.at[c], fsem.at[i]) for i, c in enumerate(cuts)]
    load_back.start()
    for cp in load_part + load_out:
        cp.start()
    wg[...] = wg_a[...]
    gg[...] = gg_a[...]
    sg[...] = sg_a[...]
    load_back.wait()
    for cp in load_part:
        cp.wait()

    @pl.loop(0, NDOM, unroll=4)
    def _(p):
        for s in range(SENT):
            b = cs[(C_LIST + s) * BLK + p]
            part[b] = part[b] + back[p * SENT + s].astype(F32)

    for i in range(4):
        load_out[i].wait()
        put_out[i].start()

        @pl.loop(i * n, (i + 1) * n, unroll=n)
        def _(b):
            made[b] = part[b].astype(BF16)

        put_fg[i].start()
    for cp in put_out + put_fg:
        cp.wait()


def fold(v):
    return jnp.sum(v.reshape(-1, 8, v.shape[-1]), axis=0)


def layer(
    cs, feat_h, tiles_h, cot_h, wself, wneigh, gain, shift, rmean, rstd,
    out_h, part_h, back_h, wg_out, gg_out, sg_out,
    tv, pool, own, st, own_back, agg, ct, inv, ost, slots, wloc, wgat, wpart, wdom, wfin, ga, da, gb, db,
    lsem, tsem, osem, fsend, frecv, bsend, brecv, gs, gr, ds, dr, w1s, w1r, w2s, w2r, w3s, w3r, w4s, w4r,
):
    d = lax.axis_index("dom")
    g = lax.axis_index("group")
    x = d // 4
    zc = d % 4

    def dpeer(off):
        return ((x + off[0]) % 4) * 4 + (zc + off[1]) % 4

    load_feat = pltpu.make_async_copy(feat_h, own, lsem.at[0])
    load_tiles = pltpu.make_async_copy(tiles_h, tv.at[pl.ds(0, NT)], tsem.at[0])
    load_cot = pltpu.make_async_copy(cot_h, ct, lsem.at[1])
    load_feat.start()
    barrier = pltpu.get_barrier_semaphore()
    for off in OFFSETS:
        pl.semaphore_signal(barrier, inc=1, device_id=(dpeer(off), g), device_id_type=MESH)
    for k in range(1, NGRP):
        pl.semaphore_signal(barrier, inc=1, device_id=(d, (g + k) % NGRP), device_id_type=MESH)
    load_feat.wait()
    load_tiles.start()
    load_cot.start()

    def forward_copy(i):
        return pltpu.make_async_remote_copy(
            src_ref=st.at[pl.ds(i * SENT, SENT)],
            dst_ref=pool.at[pl.ds(NB + d * SENT, SENT)],
            send_sem=fsend.at[i],
            recv_sem=frecv.at[i],
            device_id=(dpeer(OFFSETS[i]), g),
            device_id_type=MESH,
        )

    def backward_copy(i):
        return pltpu.make_async_remote_copy(
            src_ref=st.at[pl.ds(i * SENT, SENT)],
            dst_ref=back_h.at[pl.ds(d * SENT, SENT)],
            send_sem=bsend.at[i],
            recv_sem=brecv.at[i],
            device_id=(dpeer(OFFSETS[i]), g),
            device_id_type=MESH,
        )

    npeers = len(OFFSETS)
    for i in range(npeers):
        p = dpeer(OFFSETS[i])
        for s in range(SENT):
            st[i * SENT + s] = own[cs[(C_LIST + s) * BLK + p]]
        if i == 0:
            pl.semaphore_wait(barrier, npeers + NGRP - 1)
        forward_copy(i).start()

    for s in range(SENT):
        pool[NB + d * SENT + s] = own[cs[(C_LIST + s) * BLK + d]]

    @pl.loop(0, NB, unroll=4)
    def _(b):
        pool[b] = own[b]

    z = slots.at[pl.ds(0, NB)]
    gy = slots.at[pl.ds(NB, NB)]
    w1 = wself[...]
    w2 = wneigh[...]

    @pl.loop(0, NB // 4)
    def _(c):
        rows = own[pl.ds(c * 4, 4)].reshape(4 * BLK, BLK)
        z[pl.ds(c * 4, 4)] = jnp.dot(rows, w1, preferred_element_type=F32).reshape(4, BLK, BLK)

    load_tiles.wait()
    ones = jnp.ones((TILES * BLK, BLK), BF16)

    @pl.loop(0, NB, unroll=4)
    def _(b):
        left = jnp.concatenate([tv[b * TILES + k] for k in range(TILES)], axis=1)
        inv[b] = 1.0 / jnp.dot(left, ones, preferred_element_type=F32)

    load_cot.wait()
    for i in range(npeers):
        forward_copy(i).wait_recv()

    @pl.loop(0, NB, unroll=17)
    def _(b):
        left = jnp.concatenate([tv[b * TILES + k] for k in range(TILES)], axis=1)
        right = jnp.concatenate([pool[cs[(C_SRC + k) * BLK + b]] for k in range(TILES)], axis=0)
        summed = jnp.dot(left, right, preferred_element_type=F32)
        agg[b] = (summed * inv[b]).astype(BF16)

    def project(c, total):
        rows = agg[pl.ds(c * 4, 4)].reshape(4 * BLK, BLK)
        zz = z[pl.ds(c * 4, 4)].reshape(4 * BLK, BLK) + jnp.dot(rows, w2, preferred_element_type=F32)
        z[pl.ds(c * 4, 4)] = zz.reshape(4, BLK, BLK)
        return total + fold(zz)

    zero8 = jnp.zeros((8, BLK), F32)
    total = lax.fori_loop(0, NB // 4, project, zero8, unroll=17)
    mean_here = row_sum(total) * (1.0 / ROWS)

    def squares(b, total):
        c = z[b] - mean_here
        return total + fold(c * c)

    square_here = row_sum(lax.fori_loop(0, NB, squares, zero8, unroll=4))

    def group_copies(n, buf):
        cps = []
        for k in range(1, NGRP):
            to = (g + k) % NGRP
            cps.append(pltpu.make_async_remote_copy(
                src_ref=buf.at[g], dst_ref=buf.at[g], send_sem=gs.at[n, k], recv_sem=gr.at[n, k],
                device_id=(d, to), device_id_type=MESH,
            ))
        return cps

    def dom_copies(n, buf):
        cps = []
        for k in range(npeers):
            cps.append(pltpu.make_async_remote_copy(
                src_ref=buf.at[d], dst_ref=buf.at[d], send_sem=ds.at[n, k], recv_sem=dr.at[n, k],
                device_id=(dpeer(OFFSETS[k]), g), device_id_type=MESH,
            ))
        return cps

    def merge(buf, count, n):
        means = jnp.sum(buf[:, 0:1, :], axis=0) * (1.0 / count)
        spread = jnp.sum((buf[:, 0:1, :] - means[None]) ** 2, axis=0)
        return means, jnp.sum(buf[:, 1:2, :], axis=0) + spread * n

    ga[g] = jnp.concatenate([mean_here, square_here], axis=0)
    ga_cps = group_copies(0, ga)
    for cp in ga_cps:
        cp.start()
    for cp in ga_cps:
        cp.wait_recv()
    mean_g, square_g = merge(ga, NGRP, float(ROWS))
    da[d] = jnp.concatenate([mean_g, square_g], axis=0)
    da_cps = dom_copies(0, da)
    for cp in da_cps:
        cp.start()
    for i in range(npeers):
        forward_copy(i).wait_send()
    for cp in ga_cps:
        cp.wait_send()
    for cp in da_cps:
        cp.wait_recv()
    mu, square_all = merge(da, NDOM, float(ROWS * NGRP))
    nodes = float(ROWS * NGRP * NDOM)
    sigma = jnp.sqrt(square_all * (1.0 / nodes) + epsilon)
    isg = 1.0 / sigma
    rs = rstd[...]
    gn = gain[...]
    ratio = jnp.clip(sigma / rs, 1.0 / clip_ratio, clip_ratio)
    offset = jnp.clip((mu - rmean[...]) / rs, -clip_shift, clip_shift)
    slope = gn * ratio
    bias = gn * offset + shift[...]

    def activate(b, sums):
        xh = (z[b] - mu) * isg
        pre = xh * slope + bias
        sg = 1.0 / (1.0 + jnp.exp(-pre))
        ost[b] = (pre * sg).astype(BF16)
        dy = ct[b].astype(F32) * sg * (1.0 + pre * (1.0 - sg))
        gy[b] = dy
        return sums[0] + fold(dy), sums[1] + fold(dy * xh)

    sum_gy, sum_gx = lax.fori_loop(0, NB, activate, (zero8, zero8), unroll=2)
    write_out = pltpu.make_async_copy(ost, out_h, osem.at[0])
    write_out.start()

    gb[g] = jnp.concatenate([row_sum(sum_gy), row_sum(sum_gx)], axis=0)
    gb_cps = group_copies(1, gb)
    for cp in gb_cps:
        cp.start()
    for cp in gb_cps:
        cp.wait_recv()
    db[d] = jnp.sum(gb[...], axis=0)
    db_cps = dom_copies(1, db)
    for cp in db_cps:
        cp.start()
    for cp in da_cps:
        cp.wait_send()
    for cp in gb_cps:
        cp.wait_send()
    write_out.wait()
    for cp in db_cps:
        cp.wait_recv()
    sums = jnp.sum(db[...], axis=0)
    sum_gy = sums[0:1]
    sum_gx = sums[1:2]
    gg_out[...] = ratio * sum_gx + offset * sum_gy
    sg_out[...] = sum_gy
    k1 = slope * isg
    k2 = k1 * sum_gy * (1.0 / nodes)
    k3 = k1 * sum_gx * (1.0 / nodes)

    @pl.loop(0, NB, unroll=17)
    def _(b):
        xh = (z[b] - mu) * isg
        dz = gy[b] * k1 - k2 - xh * k3
        hi = dz.astype(BF16)
        ct[b] = hi
        ost[b] = (dz - hi.astype(F32)).astype(BF16)
        dagg = lax.dot_general(hi, w2, (((1,), (1,)), ((), ())), preferred_element_type=F32)
        pool[b] = (dagg * inv[b]).astype(BF16)

    pool[NB] = jnp.zeros((BLK, BLK), BF16)
    tv[NT] = jnp.zeros((BLK, BLK), BF16)

    def pair(p, acc):
        which = [cs[C_TILE * BLK + 2 * p + j] for j in range(2)]
        left = jnp.concatenate([tv[t] for t in which], axis=0)
        right = jnp.concatenate([pool[lax.shift_right_logical(t, 3)] for t in which], axis=0)
        part = lax.dot_general(left, right, (((0,), (0,)), ((), ())), preferred_element_type=F32)
        acc = acc * cs[C_KEEP * BLK + p].astype(F32) + part
        slots[p] = acc
        return acc

    lax.fori_loop(0, PAIRS_REMOTE, pair, jnp.zeros((BLK, BLK), F32), unroll=38)

    def ended(q):
        e = cs[C_END * BLK + q]
        return jnp.where(e >= 0, slots[jnp.maximum(e, 0)], 0.0)

    for i in range(npeers):
        p = dpeer(OFFSETS[i])
        for s in range(SENT):
            st[i * SENT + s] = ended(p * SENT + s).astype(BF16)
        if i < 5:
            backward_copy(i).start()
    for s in range(SENT):
        own_back[s] = ended(d * SENT + s).astype(BF16)
    put_own = pltpu.make_async_copy(own_back, back_h.at[pl.ds(d * SENT, SENT)], lsem.at[1])
    put_own.start()

    def weight(c, acc):
        left = jnp.concatenate(
            [own[pl.ds(c * 4, 4)].reshape(4 * BLK, BLK), agg[pl.ds(c * 4, 4)].reshape(4 * BLK, BLK)], axis=1
        )
        right = jnp.concatenate(
            [ct[pl.ds(c * 4, 4)].reshape(4 * BLK, BLK), ost[pl.ds(c * 4, 4)].reshape(4 * BLK, BLK)], axis=1
        )
        wloc[...] += lax.dot_general(left, right, (((0,), (0,)), ((), ())), preferred_element_type=F32)
        return acc

    wloc[...] = jnp.zeros_like(wloc)
    lax.fori_loop(0, NB // 4, weight, 0)
    part = 2 * BLK // NGRP
    wsum = wloc[:, :BLK] + wloc[:, BLK:]
    wloc[:, :BLK] = wsum
    w1_cps = []
    for k in range(1, NGRP):
        to = (g + k) % NGRP
        w1_cps.append(pltpu.make_async_remote_copy(
            src_ref=wloc.at[pl.ds(to * part, part), pl.ds(0, BLK)], dst_ref=wgat.at[g], send_sem=w1s.at[k], recv_sem=w1r.at[k],
            device_id=(d, to), device_id_type=MESH,
        ))
    for cp in w1_cps:
        cp.start()
    wgat[g] = wloc[pl.ds(g * part, part), pl.ds(0, BLK)]

    lax.fori_loop(PAIRS_REMOTE, PAIRS, pair, slots[PAIRS_REMOTE - 1], unroll=17)

    def spread(src, dst, send, recv):
        return [
            pltpu.make_async_remote_copy(
                src_ref=src(dpeer(OFFSETS[k])), dst_ref=dst, send_sem=send.at[k], recv_sem=recv.at[k],
                device_id=(dpeer(OFFSETS[k]), g), device_id_type=MESH,
            )
            for k in range(npeers)
        ]

    for cp in w1_cps:
        cp.wait_recv()
    here = jnp.sum(wgat[...], axis=0)
    for i in range(NDOM):
        wpart[i] = here[2 * i : 2 * i + 2]
    wdom[d] = wpart[d]
    w2_cps = spread(lambda p: wpart.at[p], wdom.at[d], w2s, w2r)
    for cp in w2_cps:
        cp.start()
    for i in range(5, 10):
        backward_copy(i).start()

    @pl.loop(0, NB, unroll=17)
    def _(b):
        dself = lax.dot_general(ct[b], w1, (((1,), (1,)), ((), ())), preferred_element_type=F32)
        inv[b] = dself + ended(NREM + b)

    put_part = pltpu.make_async_copy(inv, part_h, osem.at[1])
    put_part.start()
    for cp in w2_cps:
        cp.wait_recv()
    wfin[d] = jnp.sum(wdom[...], axis=0)
    w3_cps = spread(lambda p: wfin.at[d], wfin.at[d], w3s, w3r)
    for cp in w3_cps:
        cp.start()
    for i in range(10, npeers):
        backward_copy(i).start()
    for cp in w3_cps:
        cp.wait_recv()
    wg_out[pl.ds(g * part, part)] = jnp.concatenate([wfin[i] for i in range(NDOM)], axis=0)
    w4_cps = []
    for k in range(1, NGRP):
        w4_cps.append(pltpu.make_async_remote_copy(
            src_ref=wg_out.at[pl.ds(g * part, part)], dst_ref=wg_out.at[pl.ds(g * part, part)],
            send_sem=w4s.at[k], recv_sem=w4r.at[k], device_id=(d, (g + k) % NGRP), device_id_type=MESH,
        ))
    for cp in w4_cps:
        cp.start()
    put_own.wait()
    put_part.wait()
    for cp in db_cps + w1_cps + w2_cps + w3_cps:
        cp.wait_send()
    for cp in w4_cps:
        cp.wait()
    for i in range(npeers):
        backward_copy(i).wait()


def on_device(features, tiles, tile_src, send_list, w_self, w_neigh, gain, shift, run_mean, run_std, cotangent):
    vm = pl.BlockSpec(memory_space=pltpu.VMEM)
    sm = pl.BlockSpec(memory_space=pltpu.SMEM)
    hb = pl.BlockSpec(memory_space=pl.ANY)
    dma = pltpu.SemaphoreType.DMA
    part = 2 * BLK // NGRP
    ctl = pl.pallas_call(
        plan,
        name="plan",
        out_shape=jax.ShapeDtypeStruct((C_ROWS, BLK), jnp.int32),
        in_specs=[vm, vm],
        out_specs=vm,
        scratch_shapes=[pltpu.VMEM((BLK, BLK), F32)],
    )(tile_src.T, send_list.reshape(NDOM, SENT).T).reshape(C_ROWS * BLK)
    results = (
        jax.ShapeDtypeStruct((NB, BLK, BLK), BF16),
        jax.ShapeDtypeStruct((NB, BLK, BLK), BF16),
        jax.ShapeDtypeStruct((2 * BLK, BLK), F32),
        jax.ShapeDtypeStruct((1, BLK), F32),
        jax.ShapeDtypeStruct((1, BLK), F32),
    )
    partial = (
        results[0],
        jax.ShapeDtypeStruct((NB, BLK, BLK), F32),
        jax.ShapeDtypeStruct((NREM, BLK, BLK), BF16),
    ) + results[2:]
    made = pl.pallas_call(
        layer,
        name="sage",
        out_shape=partial,
        in_specs=[sm, hb, hb, hb] + [vm] * 6,
        out_specs=(hb, hb, hb, vm, vm, vm),
        scratch_shapes=[
            pltpu.VMEM((NT + 1, BLK, BLK), BF16),
            pltpu.VMEM((NPOOL, BLK, BLK), BF16),
            pltpu.VMEM((NB, BLK, BLK), BF16),
            pltpu.VMEM((NREM, BLK, BLK), BF16),
            pltpu.VMEM((SENT, BLK, BLK), BF16),
            pltpu.VMEM((NB, BLK, BLK), BF16),
            pltpu.VMEM((NB, BLK, BLK), BF16),
            pltpu.VMEM((NB, BLK, BLK), F32),
            pltpu.VMEM((NB, BLK, BLK), BF16),
            pltpu.VMEM((PAIRS, BLK, BLK), F32),
            pltpu.VMEM((2 * BLK, 2 * BLK), F32),
            pltpu.VMEM((NGRP, part, BLK), F32),
            pltpu.VMEM((NDOM, 2, BLK), F32),
            pltpu.VMEM((NDOM, 2, BLK), F32),
            pltpu.VMEM((NDOM, 2, BLK), F32),
            pltpu.VMEM((NGRP, 2, BLK), F32),
            pltpu.VMEM((NDOM, 2, BLK), F32),
            pltpu.VMEM((NGRP, 2, BLK), F32),
            pltpu.VMEM((NDOM, 2, BLK), F32),
            dma((2,)), dma((1,)), dma((2,)),
            dma((15,)), dma((15,)), dma((15,)), dma((15,)),
            dma((2, 8)), dma((2, 8)), dma((2, 15)), dma((2, 15)),
            dma((8,)), dma((8,)), dma((15,)), dma((15,)), dma((15,)), dma((15,)), dma((8,)), dma((8,)),
        ],
        compiler_params=pltpu.CompilerParams(
            collective_id=1, has_side_effects=True, vmem_limit_bytes=63 * 1024 * 1024
        ),
    )(
        ctl,
        features.reshape(NB, BLK, BLK), tiles.reshape(NT, BLK, BLK), cotangent.reshape(NB, BLK, BLK),
        w_self, w_neigh, gain.reshape(1, BLK), shift.reshape(1, BLK), run_mean.reshape(1, BLK), run_std.reshape(1, BLK),
    )
    out, fg, wg, gg, sg = pl.pallas_call(
        finish,
        name="finish",
        out_shape=results,
        in_specs=[sm, hb, hb, hb, vm, vm, vm],
        out_specs=(hb, hb, vm, vm, vm),
        scratch_shapes=[
            pltpu.VMEM((NB, BLK, BLK), BF16),
            pltpu.VMEM((NB, BLK, BLK), F32),
            pltpu.VMEM((NREM, BLK, BLK), BF16),
            pltpu.VMEM((NB, BLK, BLK), BF16),
            dma((4,)), dma((1,)), dma((4,)), dma((4,)), dma((4,)),
        ],
        compiler_params=pltpu.CompilerParams(vmem_limit_bytes=63 * 1024 * 1024),
    )(ctl, *made)
    return out.reshape(ROWS, BLK), fg.reshape(ROWS, BLK), wg, gg.reshape(BLK), sg.reshape(BLK)


def solution(mesh):
    rows = P(("dom", "group"), None)
    return jax.shard_map(
        on_device,
        mesh=mesh,
        in_specs=(
            rows,
            P(("dom", "group"), None, None, None),
            rows,
            P("dom", "group", None, None),
            P(), P(), P(), P(), P(), P(),
            rows,
        ),
        out_specs=(rows, rows, P(), P(), P()),
        check_vma=False,
    )
```

```python
import functools

import jax
import jax.numpy as jnp
from jax import lax
from jax.experimental import pallas as pl
from jax.experimental.pallas import tpu as pltpu
from jax.sharding import PartitionSpec as P

BLK = 128
TILES = 8
NB = 68
SENT = 4
NDOM = 16
NGRP = 8
NREM = NDOM * SENT
NT = NB * TILES
NPOOL = NB + NREM
PAIRS_REMOTE = (NT + NREM) // 2
PAIRS = (NT + NPOOL) // 2
POS_ROWS = 6
SEG = 256
ROWS = NB * BLK
MESH = pl.DeviceIdType.MESH
F32 = jnp.float32
BF16 = jnp.bfloat16

epsilon = 1e-05
clip_ratio = 2.0
clip_shift = 1.0

OFFSETS = (
    (2, 2), (2, 1), (1, 2), (2, 3), (3, 2), (1, 1), (3, 3), (1, 3),
    (3, 1), (2, 0), (0, 2), (1, 0), (0, 1), (3, 0), (0, 3),
)

C_TILE, C_KEEP, C_END = 0, 6, 9
C_ROWS = 16


def iota(shape, dim):
    return lax.broadcasted_iota(jnp.int32, shape, dim)


def lane_sum(v):
    return jnp.sum(v, axis=1, keepdims=True)


def row_sum(v):
    return jnp.sum(v, axis=0, keepdims=True)


def one(mask):
    return jnp.where(mask, 1, 0)


def put_rows(ctl, first, values):
    width = values.shape[1]
    for i in range(width // BLK):
        ctl[first + i : first + i + 1, :] = values[:, i * BLK : (i + 1) * BLK]


def plan(srct, ctl, wide):
    s = srct[...]
    wide[...] = jnp.full(wide.shape, 1000, jnp.int32)
    wide[0:TILES, 0:NB] = jnp.where(s >= NB, s - NB, s + NREM)
    st = wide[...]
    s = st.T
    cols = [s[:, k : k + 1] for k in range(TILES)]
    rows = [st[k : k + 1, :] for k in range(TILES)]
    lanes = iota((BLK, SEG), 1)
    counts_row = row_sum(sum(one(c == lanes) for c in cols))
    subl = iota((SEG, BLK), 0)
    counts_col = lane_sum(sum(one(r == subl) for r in rows))
    pairs_row = lax.shift_right_logical(counts_row + 1, 1)
    pairs_col = lax.shift_right_logical(counts_col + 1, 1)
    up = iota((SEG, SEG), 0)
    across = iota((SEG, SEG), 1)
    start_row = row_sum(jnp.where(up < across, pairs_col, 0))
    start_col = lane_sum(jnp.where(across < up, pairs_row, 0))
    earlier = iota((BLK, BLK), 1) < iota((BLK, BLK), 0)
    node = iota((BLK, POS_ROWS * BLK), 0)
    spot = iota((BLK, POS_ROWS * BLK), 1)
    held = jnp.zeros((BLK, POS_ROWS * BLK), jnp.int32)
    for k in range(TILES):
        same = one((rows[k] == cols[k]) & earlier)
        for j in range(k):
            same = same + one(rows[j] == cols[k])
        start = lane_sum(jnp.where(cols[k] == lanes, start_row, 0))
        place = jnp.where(cols[k] < SEG, start * 2 + lane_sum(same), -1)
        held = held + jnp.where(place == spot, node * TILES + (k + 1), 0)
    held = row_sum(held)
    put_rows(ctl, C_TILE, jnp.where(held > 0, held - 1, NT))
    spots = iota((SEG, 3 * BLK), 1)
    first = row_sum(jnp.where((start_col == spots) & (counts_col > 0), 1, 0))
    put_rows(ctl, C_KEEP, 1 - first)
    put_rows(ctl, C_END, jnp.where(counts_row > 0, start_row + pairs_row - 1, -1))


def finish(
    list_a, out_a, part_a, back_a, wg_a, gg_a, sg_a, out, fg, wg, gg, sg,
    cs, wv, gv, sv, held, part, back, made, extra, psem, bsem, isem, osem, fsem, ssem, tsem,
):
    n = NB // 4
    cuts = [pl.ds(i * n, n) for i in range(4)]
    load_ctl = pltpu.make_async_copy(list_a, cs, bsem.at[1])
    load_back = pltpu.make_async_copy(back_a, back, bsem.at[0])
    load_part = [pltpu.make_async_copy(part_a.at[c], part.at[c], psem.at[i]) for i, c in enumerate(cuts)]
    load_out = [pltpu.make_async_copy(out_a.at[c], held.at[c], isem.at[i]) for i, c in enumerate(cuts)]
    put_out = [pltpu.make_async_copy(held.at[c], out.at[c], osem.at[i]) for i, c in enumerate(cuts)]
    put_fg = [pltpu.make_async_copy(made.at[c], fg.at[c], fsem.at[i]) for i, c in enumerate(cuts)]
    small = ((wg_a, wv, wg), (gg_a, gv, gg), (sg_a, sv, sg))
    load_small = [pltpu.make_async_copy(src, mid, ssem.at[i]) for i, (src, mid, _) in enumerate(small)]
    put_small = [pltpu.make_async_copy(mid, dst, tsem.at[i]) for i, (_, mid, dst) in enumerate(small)]
    for cp in [load_ctl, load_back] + load_small + load_part + load_out:
        cp.start()

    @pl.loop(0, NB, unroll=17)
    def _(b):
        extra[b] = jnp.zeros((BLK, BLK), F32)

    for load, put in zip(load_small, put_small):
        load.wait()
        put.start()
    load_ctl.wait()
    load_back.wait()

    @pl.loop(0, NDOM, unroll=4)
    def _(p):
        for s in range(SENT):
            b = cs[s, p]
            extra[b] = extra[b] + back[p * SENT + s].astype(F32)

    for i in range(4):
        load_part[i].wait()

        @pl.loop(i * n, (i + 1) * n, unroll=n)
        def _(b):
            made[b] = (part[b] + extra[b]).astype(BF16)

        put_fg[i].start()
        load_out[i].wait()
        put_out[i].start()
    for cp in put_small + put_out + put_fg:
        cp.wait()


def fold(v):
    return jnp.sum(v.reshape(-1, 8, v.shape[-1]), axis=0)


def layer(
    src_s, list_s, src_v, feat_h, tiles_h, cot_h, wself, wneigh, gain, shift, rmean, rstd,
    out_h, part_h, back_h, wg_out, gg_out, sg_out,
    tv, pool, own, st, own_back, agg, ct, inv, ost, slots, ctl, wide, cs, wloc, wgat, wpart, wdom, wfin, ga, da, gb, db,
    lsem, tsem, osem, fsend, frecv, bsend, brecv, gs, gr, ds, dr, w1s, w1r, w2s, w2r, w3s, w3r, w4s, w4r,
):
    d = lax.axis_index("dom")
    g = lax.axis_index("group")
    x = d // 4
    zc = d % 4

    def dpeer(off):
        return ((x + off[0]) % 4) * 4 + (zc + off[1]) % 4

    load_feat = pltpu.make_async_copy(feat_h, own, lsem.at[0])
    cuts = [pl.ds(i * (NT // 4), NT // 4) for i in range(4)]
    load_tiles = [pltpu.make_async_copy(tiles_h.at[c], tv.at[c], tsem.at[i]) for i, c in enumerate(cuts)]
    load_cot = pltpu.make_async_copy(cot_h, ct, lsem.at[1])
    load_feat.start()
    barrier = pltpu.get_barrier_semaphore()
    for off in OFFSETS:
        pl.semaphore_signal(barrier, inc=1, device_id=(dpeer(off), g), device_id_type=MESH)
    for k in range(1, NGRP):
        pl.semaphore_signal(barrier, inc=1, device_id=(d, (g + k) % NGRP), device_id_type=MESH)
    load_feat.wait()

    def forward_copy(i):
        return pltpu.make_async_remote_copy(
            src_ref=st.at[pl.ds(i * SENT, SENT)],
            dst_ref=pool.at[pl.ds(NB + d * SENT, SENT)],
            send_sem=fsend.at[i],
            recv_sem=frecv.at[i],
            device_id=(dpeer(OFFSETS[i]), g),
            device_id_type=MESH,
        )

    def backward_copy(i):
        return pltpu.make_async_remote_copy(
            src_ref=st.at[pl.ds(i * SENT, SENT)],
            dst_ref=back_h.at[pl.ds(d * SENT, SENT)],
            send_sem=bsend.at[i],
            recv_sem=brecv.at[i],
            device_id=(dpeer(OFFSETS[i]), g),
            device_id_type=MESH,
        )

    npeers = len(OFFSETS)
    for i in range(npeers):
        p = dpeer(OFFSETS[i])
        for s in range(SENT):
            st[i * SENT + s] = own[list_s[s, p]]
        if i == 0:
            pl.semaphore_wait(barrier, npeers + NGRP - 1)
        forward_copy(i).start()
        if i % 3 == 2 and i // 3 < 4:
            load_tiles[i // 3].start()
    load_cot.start()

    for s in range(SENT):
        pool[NB + d * SENT + s] = own[list_s[s, d]]

    @pl.loop(0, NB, unroll=4)
    def _(b):
        pool[b] = own[b]

    plan(src_v, ctl, wide)
    ctl_copy = pltpu.make_async_copy(ctl, cs, lsem.at[2])
    ctl_copy.start()
    z = slots.at[pl.ds(0, NB)]
    gy = slots.at[pl.ds(NB, NB)]
    w1 = wself[...]
    w2 = wneigh[...]

    @pl.loop(0, NB // 4)
    def _(c):
        rows = own[pl.ds(c * 4, 4)].reshape(4 * BLK, BLK)
        z[pl.ds(c * 4, 4)] = jnp.dot(rows, w1, preferred_element_type=F32).reshape(4, BLK, BLK)

    ones = jnp.ones((TILES * BLK, BLK), BF16)
    for i in range(4):
        load_tiles[i].wait()

        @pl.loop(i * (NB // 4), (i + 1) * (NB // 4), unroll=17)
        def _(b):
            left = jnp.concatenate([tv[b * TILES + k] for k in range(TILES)], axis=1)
            inv[b] = 1.0 / jnp.dot(left, ones, preferred_element_type=F32)

    ctl_copy.wait()
    load_cot.wait()
    for i in range(npeers):
        forward_copy(i).wait_recv()

    @pl.loop(0, NB, unroll=34)
    def _(b):
        left = jnp.concatenate([tv[b * TILES + k] for k in range(TILES)], axis=1)
        right = jnp.concatenate([pool[src_s[k, b]] for k in range(TILES)], axis=0)
        summed = jnp.dot(left, right, preferred_element_type=F32)
        agg[b] = (summed * inv[b]).astype(BF16)

    def project(c, total):
        rows = agg[pl.ds(c * 4, 4)].reshape(4 * BLK, BLK)
        zz = z[pl.ds(c * 4, 4)].reshape(4 * BLK, BLK) + jnp.dot(rows, w2, preferred_element_type=F32)
        z[pl.ds(c * 4, 4)] = zz.reshape(4, BLK, BLK)
        return total + fold(zz)

    zero8 = jnp.zeros((8, BLK), F32)
    total = lax.fori_loop(0, NB // 4, project, zero8, unroll=17)
    mean_here = row_sum(total) * (1.0 / ROWS)

    def squares(b, total):
        c = z[b] - mean_here
        return total + fold(c * c)

    square_here = row_sum(lax.fori_loop(0, NB, squares, zero8, unroll=4))

    def group_copies(n, buf):
        cps = []
        for k in range(1, NGRP):
            to = (g + k) % NGRP
            cps.append(pltpu.make_async_remote_copy(
                src_ref=buf.at[g], dst_ref=buf.at[g], send_sem=gs.at[n, k], recv_sem=gr.at[n, k],
                device_id=(d, to), device_id_type=MESH,
            ))
        return cps

    def dom_copies(n, buf):
        cps = []
        for k in range(npeers):
            cps.append(pltpu.make_async_remote_copy(
                src_ref=buf.at[d], dst_ref=buf.at[d], send_sem=ds.at[n, k], recv_sem=dr.at[n, k],
                device_id=(dpeer(OFFSETS[k]), g), device_id_type=MESH,
            ))
        return cps

    def merge(buf, count, n):
        means = jnp.sum(buf[:, 0:1, :], axis=0) * (1.0 / count)
        spread = jnp.sum((buf[:, 0:1, :] - means[None]) ** 2, axis=0)
        return means, jnp.sum(buf[:, 1:2, :], axis=0) + spread * n

    ga[g] = jnp.concatenate([mean_here, square_here], axis=0)
    ga_cps = group_copies(0, ga)
    for cp in ga_cps:
        cp.start()
    for cp in ga_cps:
        cp.wait_recv()
    mean_g, square_g = merge(ga, NGRP, float(ROWS))
    da[d] = jnp.concatenate([mean_g, square_g], axis=0)
    da_cps = dom_copies(0, da)
    for cp in da_cps:
        cp.start()
    for i in range(npeers):
        forward_copy(i).wait_send()
    for cp in ga_cps:
        cp.wait_send()
    for cp in da_cps:
        cp.wait_recv()
    mu, square_all = merge(da, NDOM, float(ROWS * NGRP))
    nodes = float(ROWS * NGRP * NDOM)
    sigma = jnp.sqrt(square_all * (1.0 / nodes) + epsilon)
    isg = 1.0 / sigma
    rs = rstd[...]
    gn = gain[...]
    ratio = jnp.clip(sigma / rs, 1.0 / clip_ratio, clip_ratio)
    offset = jnp.clip((mu - rmean[...]) / rs, -clip_shift, clip_shift)
    slope = gn * ratio
    bias = gn * offset + shift[...]

    def activate(b, sums):
        xh = (z[b] - mu) * isg
        pre = xh * slope + bias
        sg = 1.0 / (1.0 + jnp.exp(-pre))
        ost[b] = (pre * sg).astype(BF16)
        dy = ct[b].astype(F32) * sg * (1.0 + pre * (1.0 - sg))
        gy[b] = dy
        return sums[0] + fold(dy), sums[1] + fold(dy * xh)

    sum_gy, sum_gx = lax.fori_loop(0, NB, activate, (zero8, zero8), unroll=2)
    write_out = pltpu.make_async_copy(ost, out_h, osem.at[0])

    gb[g] = jnp.concatenate([row_sum(sum_gy), row_sum(sum_gx)], axis=0)
    gb_cps = group_copies(1, gb)
    for cp in gb_cps:
        cp.start()
    for cp in gb_cps:
        cp.wait_recv()
    db[d] = jnp.sum(gb[...], axis=0)
    db_cps = dom_copies(1, db)
    for cp in db_cps:
        cp.start()
    write_out.start()
    for cp in da_cps:
        cp.wait_send()
    for cp in gb_cps:
        cp.wait_send()
    write_out.wait()
    for cp in db_cps:
        cp.wait_recv()
    sums = jnp.sum(db[...], axis=0)
    sum_gy = sums[0:1]
    sum_gx = sums[1:2]
    gg_out[...] = ratio * sum_gx + offset * sum_gy
    sg_out[...] = sum_gy
    k1 = slope * isg
    k2 = k1 * sum_gy * (1.0 / nodes)
    k3 = k1 * sum_gx * (1.0 / nodes)

    wloc[...] = jnp.zeros_like(wloc)

    @pl.loop(0, NB // 4, unroll=17)
    def _(c):
        his, los = [], []
        for i in range(4):
            b = c * 4 + i
            xh = (z[b] - mu) * isg
            dz = gy[b] * k1 - k2 - xh * k3
            hi = dz.astype(BF16)
            ct[b] = hi
            his.append(hi)
            los.append((dz - hi.astype(F32)).astype(BF16))
            dagg = lax.dot_general(hi, w2, (((1,), (1,)), ((), ())), preferred_element_type=F32)
            pool[b] = (dagg * inv[b]).astype(BF16)
        left = jnp.concatenate(
            [own[pl.ds(c * 4, 4)].reshape(4 * BLK, BLK), agg[pl.ds(c * 4, 4)].reshape(4 * BLK, BLK)], axis=1
        )
        right = jnp.concatenate([jnp.concatenate(his, axis=0), jnp.concatenate(los, axis=0)], axis=1)
        wloc[...] += lax.dot_general(left, right, (((0,), (0,)), ((), ())), preferred_element_type=F32)

    part = 2 * BLK // NGRP
    wloc[:, :BLK] = wloc[:, :BLK] + wloc[:, BLK:]
    w1_cps = []
    for k in range(1, NGRP):
        to = (g + k) % NGRP
        w1_cps.append(pltpu.make_async_remote_copy(
            src_ref=wloc.at[pl.ds(to * part, part), pl.ds(0, BLK)], dst_ref=wgat.at[g], send_sem=w1s.at[k], recv_sem=w1r.at[k],
            device_id=(d, to), device_id_type=MESH,
        ))
    for cp in w1_cps:
        cp.start()
    wgat[g] = wloc[pl.ds(g * part, part), pl.ds(0, BLK)]
    pool[NB] = jnp.zeros((BLK, BLK), BF16)
    tv[NT] = jnp.zeros((BLK, BLK), BF16)

    def spread(src, dst, send, recv):
        return [
            pltpu.make_async_remote_copy(
                src_ref=src(dpeer(OFFSETS[k])), dst_ref=dst, send_sem=send.at[k], recv_sem=recv.at[k],
                device_id=(dpeer(OFFSETS[k]), g), device_id_type=MESH,
            )
            for k in range(npeers)
        ]

    def pair(p, acc):
        which = [cs[C_TILE + lax.shift_right_logical(p, 6), (2 * p + j) % BLK] for j in range(2)]
        left = jnp.concatenate([tv[t] for t in which], axis=0)
        right = jnp.concatenate([pool[lax.shift_right_logical(t, 3)] for t in which], axis=0)
        part = lax.dot_general(left, right, (((0,), (0,)), ((), ())), preferred_element_type=F32)
        acc = acc * cs[C_KEEP + lax.shift_right_logical(p, 7), p % BLK].astype(F32) + part
        slots[p] = acc
        return acc

    half = PAIRS_REMOTE // 2
    acc = lax.fori_loop(0, half, pair, jnp.zeros((BLK, BLK), F32), unroll=38)
    for cp in w1_cps:
        cp.wait_recv()
    here = jnp.sum(wgat[...], axis=0)
    for i in range(NDOM):
        wpart[i] = here[2 * i : 2 * i + 2]
    wdom[d] = wpart[d]
    w2_cps = spread(lambda p: wpart.at[p], wdom.at[d], w2s, w2r)
    for cp in w2_cps:
        cp.start()
    acc = lax.fori_loop(half, PAIRS_REMOTE, pair, acc, unroll=38)

    def ended(q):
        e = cs[C_END + q // BLK, q % BLK]
        return jnp.where(e >= 0, slots[jnp.maximum(e, 0)], 0.0)

    for i in range(npeers):
        p = dpeer(OFFSETS[i])
        for s in range(SENT):
            st[i * SENT + s] = ended(p * SENT + s).astype(BF16)
        backward_copy(i).start()
        if i == 5:
            for cp in w2_cps:
                cp.wait_recv()
            wfin[d] = jnp.sum(wdom[...], axis=0)
            w3_cps = spread(lambda p: wfin.at[d], wfin.at[d], w3s, w3r)
            for cp in w3_cps:
                cp.start()
    for s in range(SENT):
        own_back[s] = ended(d * SENT + s).astype(BF16)
    put_own = pltpu.make_async_copy(own_back, back_h.at[pl.ds(d * SENT, SENT)], lsem.at[1])
    put_own.start()

    lax.fori_loop(PAIRS_REMOTE, PAIRS, pair, acc, unroll=17)

    @pl.loop(0, NB, unroll=17)
    def _(b):
        dself = lax.dot_general(ct[b], w1, (((1,), (1,)), ((), ())), preferred_element_type=F32)
        inv[b] = dself + ended(NREM + b)

    put_part = pltpu.make_async_copy(inv, part_h, osem.at[1])
    put_part.start()
    for cp in w3_cps:
        cp.wait_recv()
    wg_out[pl.ds(g * part, part)] = jnp.concatenate([wfin[i] for i in range(NDOM)], axis=0)
    w4_cps = []
    for k in range(1, NGRP):
        w4_cps.append(pltpu.make_async_remote_copy(
            src_ref=wg_out.at[pl.ds(g * part, part)], dst_ref=wg_out.at[pl.ds(g * part, part)],
            send_sem=w4s.at[k], recv_sem=w4r.at[k], device_id=(d, (g + k) % NGRP), device_id_type=MESH,
        ))
    for cp in w4_cps:
        cp.start()
    put_own.wait()
    put_part.wait()
    for cp in db_cps + w1_cps + w2_cps + w3_cps:
        cp.wait_send()
    for cp in w4_cps:
        cp.wait()
    for i in range(npeers):
        backward_copy(i).wait()


def on_device(features, tiles, tile_src, send_list, w_self, w_neigh, gain, shift, run_mean, run_std, cotangent):
    vm = pl.BlockSpec(memory_space=pltpu.VMEM)
    sm = pl.BlockSpec(memory_space=pltpu.SMEM)
    hb = pl.BlockSpec(memory_space=pl.ANY)
    dma = pltpu.SemaphoreType.DMA
    part = 2 * BLK // NGRP
    source = tile_src.T
    lists = send_list.reshape(NDOM, SENT).T
    results = (
        jax.ShapeDtypeStruct((NB, BLK, BLK), BF16),
        jax.ShapeDtypeStruct((NB, BLK, BLK), BF16),
        jax.ShapeDtypeStruct((2 * BLK, BLK), F32),
        jax.ShapeDtypeStruct((1, BLK), F32),
        jax.ShapeDtypeStruct((1, BLK), F32),
    )
    partial = (
        results[0],
        jax.ShapeDtypeStruct((NB, BLK, BLK), F32),
        jax.ShapeDtypeStruct((NREM, BLK, BLK), BF16),
    ) + results[2:]
    made = pl.pallas_call(
        layer,
        name="sage",
        out_shape=partial,
        in_specs=[sm, sm, vm, hb, hb, hb] + [vm] * 6,
        out_specs=(hb, hb, hb, vm, vm, vm),
        scratch_shapes=[
            pltpu.VMEM((NT + 1, BLK, BLK), BF16),
            pltpu.VMEM((NPOOL, BLK, BLK), BF16),
            pltpu.VMEM((NB, BLK, BLK), BF16),
            pltpu.VMEM((NREM, BLK, BLK), BF16),
            pltpu.VMEM((SENT, BLK, BLK), BF16),
            pltpu.VMEM((NB, BLK, BLK), BF16),
            pltpu.VMEM((NB, BLK, BLK), BF16),
            pltpu.VMEM((NB, BLK, BLK), F32),
            pltpu.VMEM((NB, BLK, BLK), BF16),
            pltpu.VMEM((PAIRS, BLK, BLK), F32),
            pltpu.VMEM((C_ROWS, BLK), jnp.int32),
            pltpu.VMEM((BLK, BLK), jnp.int32),
            pltpu.SMEM((C_ROWS, BLK), jnp.int32),
            pltpu.VMEM((2 * BLK, 2 * BLK), F32),
            pltpu.VMEM((NGRP, part, BLK), F32),
            pltpu.VMEM((NDOM, 2, BLK), F32),
            pltpu.VMEM((NDOM, 2, BLK), F32),
            pltpu.VMEM((NDOM, 2, BLK), F32),
            pltpu.VMEM((NGRP, 2, BLK), F32),
            pltpu.VMEM((NDOM, 2, BLK), F32),
            pltpu.VMEM((NGRP, 2, BLK), F32),
            pltpu.VMEM((NDOM, 2, BLK), F32),
            dma((3,)), dma((4,)), dma((2,)),
            dma((15,)), dma((15,)), dma((15,)), dma((15,)),
            dma((2, 8)), dma((2, 8)), dma((2, 15)), dma((2, 15)),
            dma((8,)), dma((8,)), dma((15,)), dma((15,)), dma((15,)), dma((15,)), dma((8,)), dma((8,)),
        ],
        compiler_params=pltpu.CompilerParams(
            collective_id=1, has_side_effects=True, vmem_limit_bytes=63 * 1024 * 1024
        ),
    )(
        source, lists, source,
        features.reshape(NB, BLK, BLK), tiles.reshape(NT, BLK, BLK), cotangent.reshape(NB, BLK, BLK),
        w_self, w_neigh, gain.reshape(1, BLK), shift.reshape(1, BLK), run_mean.reshape(1, BLK), run_std.reshape(1, BLK),
    )
    out, fg, wg, gg, sg = pl.pallas_call(
        finish,
        name="finish",
        out_shape=results,
        in_specs=[hb] * 7,
        out_specs=(hb,) * 5,
        scratch_shapes=[
            pltpu.SMEM((SENT, NDOM), jnp.int32),
            pltpu.VMEM((2 * BLK, BLK), F32),
            pltpu.VMEM((1, BLK), F32),
            pltpu.VMEM((1, BLK), F32),
            pltpu.VMEM((NB, BLK, BLK), BF16),
            pltpu.VMEM((NB, BLK, BLK), F32),
            pltpu.VMEM((NREM, BLK, BLK), BF16),
            pltpu.VMEM((NB, BLK, BLK), BF16),
            pltpu.VMEM((NB, BLK, BLK), F32),
            dma((4,)), dma((2,)), dma((4,)), dma((4,)), dma((4,)), dma((3,)), dma((3,)),
        ],
        compiler_params=pltpu.CompilerParams(vmem_limit_bytes=63 * 1024 * 1024),
    )(lists, *made)
    return out.reshape(ROWS, BLK), fg.reshape(ROWS, BLK), wg, gg.reshape(BLK), sg.reshape(BLK)


def solution(mesh):
    rows = P(("dom", "group"), None)
    return jax.shard_map(
        on_device,
        mesh=mesh,
        in_specs=(
            rows,
            P(("dom", "group"), None, None, None),
            rows,
            P("dom", "group", None, None),
            P(), P(), P(), P(), P(), P(),
            rows,
        ),
        out_specs=(rows, rows, P(), P(), P()),
        check_vma=False,
    )
```

```python
import functools

import jax
import jax.numpy as jnp
from jax import lax
from jax.experimental import pallas as pl
from jax.experimental.pallas import tpu as pltpu
from jax.sharding import PartitionSpec as P

BLK = 128
TILES = 8
NB = 68
SENT = 4
NDOM = 16
NGRP = 8
NREM = NDOM * SENT
NT = NB * TILES
NPOOL = NB + NREM
PAIRS_REMOTE = (NT + NREM) // 2
PAIRS = (NT + NPOOL) // 2
POS_ROWS = 6
SEG = 256
ROWS = NB * BLK
MESH = pl.DeviceIdType.MESH
F32 = jnp.float32
BF16 = jnp.bfloat16

epsilon = 1e-05
clip_ratio = 2.0
clip_shift = 1.0

OFFSETS = (
    (2, 2), (2, 1), (1, 2), (2, 3), (3, 2), (1, 1), (3, 3), (1, 3),
    (3, 1), (2, 0), (0, 2), (1, 0), (0, 1), (3, 0), (0, 3),
)

C_TILE, C_KEEP, C_END = 0, 6, 9
C_ROWS = 16


def iota(shape, dim):
    return lax.broadcasted_iota(jnp.int32, shape, dim)


def lane_sum(v):
    return jnp.sum(v, axis=1, keepdims=True)


def row_sum(v):
    return jnp.sum(v, axis=0, keepdims=True)


def one(mask):
    return jnp.where(mask, 1, 0)


def put_rows(ctl, first, values):
    width = values.shape[1]
    for i in range(width // BLK):
        ctl[first + i : first + i + 1, :] = values[:, i * BLK : (i + 1) * BLK]


def plan(srct, ctl, wide):
    s = srct[...]
    wide[...] = jnp.full(wide.shape, 1000, jnp.int32)
    wide[0:TILES, 0:NB] = jnp.where(s >= NB, s - NB, s + NREM)
    st = wide[...]
    s = st.T
    cols = [s[:, k : k + 1] for k in range(TILES)]
    rows = [st[k : k + 1, :] for k in range(TILES)]
    lanes = iota((BLK, SEG), 1)
    counts_row = row_sum(sum(one(c == lanes) for c in cols))
    subl = iota((SEG, BLK), 0)
    counts_col = lane_sum(sum(one(r == subl) for r in rows))
    pairs_row = lax.shift_right_logical(counts_row + 1, 1)
    pairs_col = lax.shift_right_logical(counts_col + 1, 1)
    up = iota((SEG, SEG), 0)
    across = iota((SEG, SEG), 1)
    start_row = row_sum(jnp.where(up < across, pairs_col, 0))
    start_col = lane_sum(jnp.where(across < up, pairs_row, 0))
    earlier = iota((BLK, BLK), 1) < iota((BLK, BLK), 0)
    node = iota((BLK, POS_ROWS * BLK), 0)
    spot = iota((BLK, POS_ROWS * BLK), 1)
    held = jnp.zeros((BLK, POS_ROWS * BLK), jnp.int32)
    for k in range(TILES):
        same = one((rows[k] == cols[k]) & earlier)
        for j in range(k):
            same = same + one(rows[j] == cols[k])
        start = lane_sum(jnp.where(cols[k] == lanes, start_row, 0))
        place = jnp.where(cols[k] < SEG, start * 2 + lane_sum(same), -1)
        held = held + jnp.where(place == spot, node * TILES + (k + 1), 0)
    held = row_sum(held)
    put_rows(ctl, C_TILE, jnp.where(held > 0, held - 1, NT))
    spots = iota((SEG, 3 * BLK), 1)
    first = row_sum(jnp.where((start_col == spots) & (counts_col > 0), 1, 0))
    put_rows(ctl, C_KEEP, 1 - first)
    put_rows(ctl, C_END, jnp.where(counts_row > 0, start_row + pairs_row - 1, -1))


def finish(
    list_a, out_a, part_a, back_a, wg_a, gg_a, sg_a, out, fg, wg, gg, sg,
    cs, wv, gv, sv, held, part, back, made, extra, psem, bsem, isem, osem, fsem, ssem, tsem,
):
    n = NB // 4
    cuts = [pl.ds(i * n, n) for i in range(4)]
    load_ctl = pltpu.make_async_copy(list_a, cs, bsem.at[1])
    load_back = pltpu.make_async_copy(back_a, back, bsem.at[0])
    load_part = [pltpu.make_async_copy(part_a.at[c], part.at[c], psem.at[i]) for i, c in enumerate(cuts)]
    load_out = [pltpu.make_async_copy(out_a.at[c], held.at[c], isem.at[i]) for i, c in enumerate(cuts)]
    put_out = [pltpu.make_async_copy(held.at[c], out.at[c], osem.at[i]) for i, c in enumerate(cuts)]
    put_fg = [pltpu.make_async_copy(made.at[c], fg.at[c], fsem.at[i]) for i, c in enumerate(cuts)]
    small = ((wg_a, wv, wg), (gg_a, gv, gg), (sg_a, sv, sg))
    load_small = [pltpu.make_async_copy(src, mid, ssem.at[i]) for i, (src, mid, _) in enumerate(small)]
    put_small = [pltpu.make_async_copy(mid, dst, tsem.at[i]) for i, (_, mid, dst) in enumerate(small)]
    for cp in [load_ctl, load_back] + load_small + load_part + load_out:
        cp.start()

    @pl.loop(0, NB, unroll=17)
    def _(b):
        extra[b] = jnp.zeros((BLK, BLK), F32)

    for load, put in zip(load_small, put_small):
        load.wait()
        put.start()
    load_ctl.wait()
    load_back.wait()

    @pl.loop(0, NDOM, unroll=4)
    def _(p):
        for s in range(SENT):
            b = cs[s, p]
            extra[b] = extra[b] + back[p * SENT + s].astype(F32)

    for i in range(4):
        load_part[i].wait()

        @pl.loop(i * n, (i + 1) * n, unroll=n)
        def _(b):
            made[b] = (part[b] + extra[b]).astype(BF16)

        put_fg[i].start()
        load_out[i].wait()
        put_out[i].start()
    for cp in put_small + put_out + put_fg:
        cp.wait()


def fold(v):
    return jnp.sum(v.reshape(-1, 8, v.shape[-1]), axis=0)


def layer(
    src_s, list_s, src_v, feat_h, tiles_h, cot_h, wself, wneigh, gain, shift, rmean, rstd,
    out_h, part_h, back_h, wg_out, gg_out, sg_out,
    tv, pool, own, st, own_back, agg, ct, inv, ost, slots, ctl, wide, cs, wloc, wgat, wpart, wdom, wfin, ga, da, gb, db,
    lsem, tsem, osem, fsend, frecv, bsend, brecv, gs, gr, ds, dr, w1s, w1r, w2s, w2r, w3s, w3r, w4s, w4r,
):
    d = lax.axis_index("dom")
    g = lax.axis_index("group")
    x = d // 4
    zc = d % 4

    def dpeer(off):
        return ((x + off[0]) % 4) * 4 + (zc + off[1]) % 4

    load_feat = pltpu.make_async_copy(feat_h, own, lsem.at[0])
    cuts = [pl.ds(i * (NT // 4), NT // 4) for i in range(4)]
    load_tiles = [pltpu.make_async_copy(tiles_h.at[c], tv.at[c], tsem.at[i]) for i, c in enumerate(cuts)]
    load_cot = pltpu.make_async_copy(cot_h, ct, lsem.at[1])
    load_feat.start()
    barrier = pltpu.get_barrier_semaphore()
    for off in OFFSETS:
        pl.semaphore_signal(barrier, inc=1, device_id=(dpeer(off), g), device_id_type=MESH)
    for k in range(1, NGRP):
        pl.semaphore_signal(barrier, inc=1, device_id=(d, (g + k) % NGRP), device_id_type=MESH)
    load_feat.wait()

    def forward_copy(i):
        return pltpu.make_async_remote_copy(
            src_ref=st.at[pl.ds(i * SENT, SENT)],
            dst_ref=pool.at[pl.ds(NB + d * SENT, SENT)],
            send_sem=fsend.at[i],
            recv_sem=frecv.at[i],
            device_id=(dpeer(OFFSETS[i]), g),
            device_id_type=MESH,
        )

    def backward_copy(i):
        return pltpu.make_async_remote_copy(
            src_ref=st.at[pl.ds(i * SENT, SENT)],
            dst_ref=back_h.at[pl.ds(d * SENT, SENT)],
            send_sem=bsend.at[i],
            recv_sem=brecv.at[i],
            device_id=(dpeer(OFFSETS[i]), g),
            device_id_type=MESH,
        )

    npeers = len(OFFSETS)
    for i in range(npeers):
        p = dpeer(OFFSETS[i])
        for s in range(SENT):
            st[i * SENT + s] = own[list_s[s, p]]
        if i == 0:
            pl.semaphore_wait(barrier, npeers + NGRP - 1)
        forward_copy(i).start()
        if i % 3 == 2 and i // 3 < 4:
            load_tiles[i // 3].start()
    load_cot.start()

    for s in range(SENT):
        pool[NB + d * SENT + s] = own[list_s[s, d]]

    @pl.loop(0, NB, unroll=4)
    def _(b):
        pool[b] = own[b]

    plan(src_v, ctl, wide)
    ctl_copy = pltpu.make_async_copy(ctl, cs, lsem.at[2])
    ctl_copy.start()
    z = slots.at[pl.ds(0, NB)]
    gy = slots.at[pl.ds(NB, NB)]
    w1 = wself[...]
    w2 = wneigh[...]

    @pl.loop(0, NB // 4)
    def _(c):
        rows = own[pl.ds(c * 4, 4)].reshape(4 * BLK, BLK)
        z[pl.ds(c * 4, 4)] = jnp.dot(rows, w1, preferred_element_type=F32).reshape(4, BLK, BLK)

    ones = jnp.ones((TILES * BLK, BLK), BF16)
    for i in range(4):
        load_tiles[i].wait()

        @pl.loop(i * (NB // 4), (i + 1) * (NB // 4), unroll=17)
        def _(b):
            left = jnp.concatenate([tv[b * TILES + k] for k in range(TILES)], axis=1)
            inv[b] = 1.0 / jnp.dot(left, ones, preferred_element_type=F32)

    ctl_copy.wait()
    load_cot.wait()
    for i in range(npeers):
        forward_copy(i).wait_recv()

    @pl.loop(0, NB, unroll=34)
    def _(b):
        left = jnp.concatenate([tv[b * TILES + k] for k in range(TILES)], axis=1)
        right = jnp.concatenate([pool[src_s[k, b]] for k in range(TILES)], axis=0)
        summed = jnp.dot(left, right, preferred_element_type=F32)
        agg[b] = (summed * inv[b]).astype(BF16)

    def project(c, total):
        rows = agg[pl.ds(c * 4, 4)].reshape(4 * BLK, BLK)
        zz = z[pl.ds(c * 4, 4)].reshape(4 * BLK, BLK) + jnp.dot(rows, w2, preferred_element_type=F32)
        z[pl.ds(c * 4, 4)] = zz.reshape(4, BLK, BLK)
        return total + fold(zz)

    zero8 = jnp.zeros((8, BLK), F32)
    total = lax.fori_loop(0, NB // 4, project, zero8, unroll=17)
    mean_here = row_sum(total) * (1.0 / ROWS)

    def squares(b, total):
        c = z[b] - mean_here
        return total + fold(c * c)

    square_here = row_sum(lax.fori_loop(0, NB, squares, zero8, unroll=4))

    def group_copies(n, buf):
        cps = []
        for k in range(1, NGRP):
            to = (g + k) % NGRP
            cps.append(pltpu.make_async_remote_copy(
                src_ref=buf.at[g], dst_ref=buf.at[g], send_sem=gs.at[n, k], recv_sem=gr.at[n, k],
                device_id=(d, to), device_id_type=MESH,
            ))
        return cps

    def dom_copies(n, buf):
        cps = []
        for k in range(npeers):
            cps.append(pltpu.make_async_remote_copy(
                src_ref=buf.at[d], dst_ref=buf.at[d], send_sem=ds.at[n, k], recv_sem=dr.at[n, k],
                device_id=(dpeer(OFFSETS[k]), g), device_id_type=MESH,
            ))
        return cps

    def merge(buf, count, n):
        means = jnp.sum(buf[:, 0:1, :], axis=0) * (1.0 / count)
        spread = jnp.sum((buf[:, 0:1, :] - means[None]) ** 2, axis=0)
        return means, jnp.sum(buf[:, 1:2, :], axis=0) + spread * n

    ga[g] = jnp.concatenate([mean_here, square_here], axis=0)
    ga_cps = group_copies(0, ga)
    for cp in ga_cps:
        cp.start()
    for cp in ga_cps:
        cp.wait_recv()
    mean_g, square_g = merge(ga, NGRP, float(ROWS))
    da[d] = jnp.concatenate([mean_g, square_g], axis=0)
    da_cps = dom_copies(0, da)
    for cp in da_cps:
        cp.start()
    for i in range(npeers):
        forward_copy(i).wait_send()
    for cp in ga_cps:
        cp.wait_send()
    for cp in da_cps:
        cp.wait_recv()
    mu, square_all = merge(da, NDOM, float(ROWS * NGRP))
    nodes = float(ROWS * NGRP * NDOM)
    sigma = jnp.sqrt(square_all * (1.0 / nodes) + epsilon)
    isg = 1.0 / sigma
    rs = rstd[...]
    gn = gain[...]
    ratio = jnp.clip(sigma / rs, 1.0 / clip_ratio, clip_ratio)
    offset = jnp.clip((mu - rmean[...]) / rs, -clip_shift, clip_shift)
    slope = gn * ratio
    bias = gn * offset + shift[...]

    def activate(b, sums):
        xh = (z[b] - mu) * isg
        pre = xh * slope + bias
        sg = 0.5 * jnp.tanh(0.5 * pre) + 0.5
        ost[b] = (pre * sg).astype(BF16)
        dy = ct[b].astype(F32) * sg * (1.0 + pre * (1.0 - sg))
        gy[b] = dy
        return sums[0] + fold(dy), sums[1] + fold(dy * xh)

    sum_gy, sum_gx = lax.fori_loop(0, NB, activate, (zero8, zero8), unroll=4)
    write_out = pltpu.make_async_copy(ost, out_h, osem.at[0])

    gb[g] = jnp.concatenate([row_sum(sum_gy), row_sum(sum_gx)], axis=0)
    gb_cps = group_copies(1, gb)
    for cp in gb_cps:
        cp.start()
    for cp in gb_cps:
        cp.wait_recv()
    db[d] = jnp.sum(gb[...], axis=0)
    db_cps = dom_copies(1, db)
    for cp in db_cps:
        cp.start()
    write_out.start()
    for cp in da_cps:
        cp.wait_send()
    for cp in gb_cps:
        cp.wait_send()
    write_out.wait()
    for cp in db_cps:
        cp.wait_recv()
    sums = jnp.sum(db[...], axis=0)
    sum_gy = sums[0:1]
    sum_gx = sums[1:2]
    gg_out[...] = ratio * sum_gx + offset * sum_gy
    sg_out[...] = sum_gy
    k1 = slope * isg
    k2 = k1 * sum_gy * (1.0 / nodes)
    k3 = k1 * sum_gx * (1.0 / nodes)

    wloc[...] = jnp.zeros_like(wloc)

    @pl.loop(0, NB // 4, unroll=17)
    def _(c):
        his, los = [], []
        for i in range(4):
            b = c * 4 + i
            xh = (z[b] - mu) * isg
            dz = gy[b] * k1 - k2 - xh * k3
            hi = dz.astype(BF16)
            ct[b] = hi
            his.append(hi)
            los.append((dz - hi.astype(F32)).astype(BF16))
            dagg = lax.dot_general(hi, w2, (((1,), (1,)), ((), ())), preferred_element_type=F32)
            pool[b] = (dagg * inv[b]).astype(BF16)
        left = jnp.concatenate(
            [own[pl.ds(c * 4, 4)].reshape(4 * BLK, BLK), agg[pl.ds(c * 4, 4)].reshape(4 * BLK, BLK)], axis=1
        )
        right = jnp.concatenate([jnp.concatenate(his, axis=0), jnp.concatenate(los, axis=0)], axis=1)
        wloc[...] += lax.dot_general(left, right, (((0,), (0,)), ((), ())), preferred_element_type=F32)

    part = 2 * BLK // NGRP
    wloc[:, :BLK] = wloc[:, :BLK] + wloc[:, BLK:]
    w1_cps = []
    for k in range(1, NGRP):
        to = (g + k) % NGRP
        w1_cps.append(pltpu.make_async_remote_copy(
            src_ref=wloc.at[pl.ds(to * part, part), pl.ds(0, BLK)], dst_ref=wgat.at[g], send_sem=w1s.at[k], recv_sem=w1r.at[k],
            device_id=(d, to), device_id_type=MESH,
        ))
    for cp in w1_cps:
        cp.start()
    wgat[g] = wloc[pl.ds(g * part, part), pl.ds(0, BLK)]
    pool[NB] = jnp.zeros((BLK, BLK), BF16)
    tv[NT] = jnp.zeros((BLK, BLK), BF16)

    def spread(src, dst, send, recv):
        return [
            pltpu.make_async_remote_copy(
                src_ref=src(dpeer(OFFSETS[k])), dst_ref=dst, send_sem=send.at[k], recv_sem=recv.at[k],
                device_id=(dpeer(OFFSETS[k]), g), device_id_type=MESH,
            )
            for k in range(npeers)
        ]

    def pair(p, acc):
        which = [cs[C_TILE + lax.shift_right_logical(p, 6), (2 * p + j) % BLK] for j in range(2)]
        left = jnp.concatenate([tv[t] for t in which], axis=0)
        right = jnp.concatenate([pool[lax.shift_right_logical(t, 3)] for t in which], axis=0)
        part = lax.dot_general(left, right, (((0,), (0,)), ((), ())), preferred_element_type=F32)
        acc = acc * cs[C_KEEP + lax.shift_right_logical(p, 7), p % BLK].astype(F32) + part
        slots[p] = acc
        return acc

    half = PAIRS_REMOTE // 2
    acc = lax.fori_loop(0, half, pair, jnp.zeros((BLK, BLK), F32), unroll=38)
    for cp in w1_cps:
        cp.wait_recv()
    here = jnp.sum(wgat[...], axis=0)
    for i in range(NDOM):
        wpart[i] = here[2 * i : 2 * i + 2]
    wdom[d] = wpart[d]
    w2_cps = spread(lambda p: wpart.at[p], wdom.at[d], w2s, w2r)
    for cp in w2_cps:
        cp.start()
    acc = lax.fori_loop(half, PAIRS_REMOTE, pair, acc, unroll=38)

    def ended(q):
        e = cs[C_END + q // BLK, q % BLK]
        return jnp.where(e >= 0, slots[jnp.maximum(e, 0)], 0.0)

    for i in range(npeers):
        p = dpeer(OFFSETS[i])
        for s in range(SENT):
            st[i * SENT + s] = ended(p * SENT + s).astype(BF16)
        backward_copy(i).start()
        if i == 5:
            for cp in w2_cps:
                cp.wait_recv()
            wfin[d] = jnp.sum(wdom[...], axis=0)
            w3_cps = spread(lambda p: wfin.at[d], wfin.at[d], w3s, w3r)
            for cp in w3_cps:
                cp.start()
    for s in range(SENT):
        own_back[s] = ended(d * SENT + s).astype(BF16)
    put_own = pltpu.make_async_copy(own_back, back_h.at[pl.ds(d * SENT, SENT)], lsem.at[1])
    put_own.start()

    lax.fori_loop(PAIRS_REMOTE, PAIRS, pair, acc, unroll=17)

    @pl.loop(0, NB, unroll=17)
    def _(b):
        dself = lax.dot_general(ct[b], w1, (((1,), (1,)), ((), ())), preferred_element_type=F32)
        inv[b] = dself + ended(NREM + b)

    put_part = pltpu.make_async_copy(inv, part_h, osem.at[1])
    put_part.start()
    for cp in w3_cps:
        cp.wait_recv()
    wg_out[pl.ds(g * part, part)] = jnp.concatenate([wfin[i] for i in range(NDOM)], axis=0)
    w4_cps = []
    for k in range(1, NGRP):
        w4_cps.append(pltpu.make_async_remote_copy(
            src_ref=wg_out.at[pl.ds(g * part, part)], dst_ref=wg_out.at[pl.ds(g * part, part)],
            send_sem=w4s.at[k], recv_sem=w4r.at[k], device_id=(d, (g + k) % NGRP), device_id_type=MESH,
        ))
    for cp in w4_cps:
        cp.start()
    put_own.wait()
    put_part.wait()
    for cp in db_cps + w1_cps + w2_cps + w3_cps:
        cp.wait_send()
    for cp in w4_cps:
        cp.wait()
    for i in range(npeers):
        backward_copy(i).wait()


def on_device(features, tiles, tile_src, send_list, w_self, w_neigh, gain, shift, run_mean, run_std, cotangent):
    vm = pl.BlockSpec(memory_space=pltpu.VMEM)
    sm = pl.BlockSpec(memory_space=pltpu.SMEM)
    hb = pl.BlockSpec(memory_space=pl.ANY)
    dma = pltpu.SemaphoreType.DMA
    part = 2 * BLK // NGRP
    source = tile_src.T
    lists = send_list.reshape(NDOM, SENT).T
    results = (
        jax.ShapeDtypeStruct((NB, BLK, BLK), BF16),
        jax.ShapeDtypeStruct((NB, BLK, BLK), BF16),
        jax.ShapeDtypeStruct((2 * BLK, BLK), F32),
        jax.ShapeDtypeStruct((1, BLK), F32),
        jax.ShapeDtypeStruct((1, BLK), F32),
    )
    partial = (
        results[0],
        jax.ShapeDtypeStruct((NB, BLK, BLK), F32),
        jax.ShapeDtypeStruct((NREM, BLK, BLK), BF16),
    ) + results[2:]
    made = pl.pallas_call(
        layer,
        name="sage",
        out_shape=partial,
        in_specs=[sm, sm, vm, hb, hb, hb] + [vm] * 6,
        out_specs=(hb, hb, hb, vm, vm, vm),
        scratch_shapes=[
            pltpu.VMEM((NT + 1, BLK, BLK), BF16),
            pltpu.VMEM((NPOOL, BLK, BLK), BF16),
            pltpu.VMEM((NB, BLK, BLK), BF16),
            pltpu.VMEM((NREM, BLK, BLK), BF16),
            pltpu.VMEM((SENT, BLK, BLK), BF16),
            pltpu.VMEM((NB, BLK, BLK), BF16),
            pltpu.VMEM((NB, BLK, BLK), BF16),
            pltpu.VMEM((NB, BLK, BLK), F32),
            pltpu.VMEM((NB, BLK, BLK), BF16),
            pltpu.VMEM((PAIRS, BLK, BLK), F32),
            pltpu.VMEM((C_ROWS, BLK), jnp.int32),
            pltpu.VMEM((BLK, BLK), jnp.int32),
            pltpu.SMEM((C_ROWS, BLK), jnp.int32),
            pltpu.VMEM((2 * BLK, 2 * BLK), F32),
            pltpu.VMEM((NGRP, part, BLK), F32),
            pltpu.VMEM((NDOM, 2, BLK), F32),
            pltpu.VMEM((NDOM, 2, BLK), F32),
            pltpu.VMEM((NDOM, 2, BLK), F32),
            pltpu.VMEM((NGRP, 2, BLK), F32),
            pltpu.VMEM((NDOM, 2, BLK), F32),
            pltpu.VMEM((NGRP, 2, BLK), F32),
            pltpu.VMEM((NDOM, 2, BLK), F32),
            dma((3,)), dma((4,)), dma((2,)),
            dma((15,)), dma((15,)), dma((15,)), dma((15,)),
            dma((2, 8)), dma((2, 8)), dma((2, 15)), dma((2, 15)),
            dma((8,)), dma((8,)), dma((15,)), dma((15,)), dma((15,)), dma((15,)), dma((8,)), dma((8,)),
        ],
        compiler_params=pltpu.CompilerParams(
            collective_id=1, has_side_effects=True, vmem_limit_bytes=63 * 1024 * 1024
        ),
    )(
        source, lists, source,
        features.reshape(NB, BLK, BLK), tiles.reshape(NT, BLK, BLK), cotangent.reshape(NB, BLK, BLK),
        w_self, w_neigh, gain.reshape(1, BLK), shift.reshape(1, BLK), run_mean.reshape(1, BLK), run_std.reshape(1, BLK),
    )
    out, fg, wg, gg, sg = pl.pallas_call(
        finish,
        name="finish",
        out_shape=results,
        in_specs=[hb] * 7,
        out_specs=(hb,) * 5,
        scratch_shapes=[
            pltpu.SMEM((SENT, NDOM), jnp.int32),
            pltpu.VMEM((2 * BLK, BLK), F32),
            pltpu.VMEM((1, BLK), F32),
            pltpu.VMEM((1, BLK), F32),
            pltpu.VMEM((NB, BLK, BLK), BF16),
            pltpu.VMEM((NB, BLK, BLK), F32),
            pltpu.VMEM((NREM, BLK, BLK), BF16),
            pltpu.VMEM((NB, BLK, BLK), BF16),
            pltpu.VMEM((NB, BLK, BLK), F32),
            dma((4,)), dma((2,)), dma((4,)), dma((4,)), dma((4,)), dma((3,)), dma((3,)),
        ],
        compiler_params=pltpu.CompilerParams(vmem_limit_bytes=63 * 1024 * 1024),
    )(lists, *made)
    return out.reshape(ROWS, BLK), fg.reshape(ROWS, BLK), wg, gg.reshape(BLK), sg.reshape(BLK)


def solution(mesh):
    rows = P(("dom", "group"), None)
    return jax.shard_map(
        on_device,
        mesh=mesh,
        in_specs=(
            rows,
            P(("dom", "group"), None, None, None),
            rows,
            P("dom", "group", None, None),
            P(), P(), P(), P(), P(), P(),
            rows,
        ),
        out_specs=(rows, rows, P(), P(), P()),
        check_vma=False,
    )
```
